512 devices in a mesh: dp: 16 (over z_hi, x, core), ctx: 32 (over y, z_lo).
Axes of the slice: x: 4, y: 8, z: 8 (z_hi: 2, z_lo: 4; z = z_hi * 4 + z_lo), core: 2. Of those that a mesh axis runs over, the one named last changes fastest.
Arguments:
- queries: bfloat16 [16, 16384, 512], P('dp', 'ctx'), may hold values from -36 to 36
- keys: bfloat16 [16, 16384, 512], P('dp', 'ctx'), may hold values from -36 to 36
- values: bfloat16 [16, 16384, 512], P('dp', 'ctx'), may hold values from -6 to 6
- grad_out: bfloat16 [16, 16384, 512], P('dp', 'ctx'), may hold values from -48 to 48
- gains: float32 [2, 512], replicated, may hold values from 0.1 to 1.9
Outputs:
- grad_queries: bfloat16 [16, 16384, 512], P('dp', 'ctx')
- grad_keys: bfloat16 [16, 16384, 512], P('dp', 'ctx')
- grad_values: bfloat16 [16, 16384, 512], P('dp', 'ctx')
- gain_grads: float32 [2, 512], P(None, 'dp')
The draws below stay inside these ranges and needn't reach their ends.
All inputs are finite; a program needn't handle non-finite values.
Results may differ from the reference program's by a relative error of at most 0.0093.
Values may be sent and summed in bfloat16 or wider, within the bound.
A program may use at most 64 MiB of HBM per device.

```python
import math
import jax
import jax.numpy as jnp
from jax import lax

HEADS = 4
HD = 128
TOK_DEV = 512
WINDOW = 512
HH = 512
SEQ = 16384
BATCH = 16


def scaled_noise(key):
    noise_key, column_key, row_key = jax.random.split(key, 3)
    column_scale = jnp.exp(jax.random.uniform(column_key, (HEADS, HD), jnp.float32, math.log(0.3), math.log(3.0)))
    row_scale = jnp.exp(jax.random.uniform(row_key, (BATCH, SEQ, HEADS, 1), jnp.float32, math.log(0.3), math.log(3.0)))
    base = jnp.clip(jax.random.normal(noise_key, (BATCH, SEQ, HEADS, HD), jnp.float32), -4.0, 4.0)
    drawn = base * column_scale * row_scale
    return drawn.reshape(BATCH, SEQ, HEADS * HD).astype(jnp.bfloat16)


def draw_queries(key, part):
    return scaled_noise(jax.random.fold_in(key, 11))


def draw_keys(key, part):
    return scaled_noise(jax.random.fold_in(key, 23))


def level_of(key, dims, pieces, low, largest):
    level = 1.0
    for dim, shards_of in pieces:
        steps = jax.random.uniform(jax.random.fold_in(jax.random.fold_in(key, 6), dim), (shards_of,), jnp.float32, low / len(pieces), largest / len(pieces))
        level = level * jnp.repeat(jnp.exp(steps), dims[dim] // shards_of).reshape((-1,) + (1,) * (len(dims) - 1 - dim))
    return level


def bell_draw(rng, dims, deviation, reach, pieces=(), kind=jnp.bfloat16):
    loudness = level_of(rng, dims, pieces, -0.22, 0.18) if pieces else 1.0
    array = jax.random.normal(rng, dims, jnp.float32) * deviation * loudness
    return jnp.minimum(jnp.maximum(array, -reach), reach).astype(kind)


def setup_inputs(seed: int = 0) -> dict:
    key_of = jax.random.split(jax.random.key(seed), 6)
    queries = draw_queries(jax.random.fold_in(key_of[5], 71), 0)
    keys = draw_keys(jax.random.fold_in(key_of[5], 71), 0)
    values = bell_draw(key_of[2], (BATCH, SEQ, HH), 1.0, 6.0, ((0, 16), (1, 32)))
    grad_out = bell_draw(key_of[3], (BATCH, SEQ, HH), 8.0, 48.0, ((0, 16), (1, 32)))
    gains = jnp.clip(1.0 + 0.18 * jax.random.normal(key_of[4], (2, HH), jnp.float32), 0.1, 1.9)
    return dict(queries=queries, keys=keys, values=values, grad_out=grad_out, gains=gains)


norm_eps = 1e-06

def unit_rows(inputs):
    count = inputs.shape[0]
    wide = inputs.astype(jnp.float32).reshape(count, HEADS, HD)
    inverse = lax.rsqrt(lax.optimization_barrier(jnp.mean(wide * wide, axis=2, keepdims=True)) + norm_eps)
    return (wide * inverse, inverse)

def norm_backward(grad_norm, unit, inverse, gain):
    count = unit.shape[0]
    grad_three = grad_norm.reshape(count, HEADS, HD)
    scaled = grad_three * gain
    mean_term = lax.optimization_barrier(jnp.mean(scaled * unit, axis=2, keepdims=True))
    grad_in = inverse * (scaled - unit * mean_term)
    gain_grad = lax.optimization_barrier(jnp.sum(grad_three * unit, axis=0)).reshape(-1)
    return (grad_in.reshape(count, HEADS * HD).astype(jnp.bfloat16), gain_grad)

def to_low(inputs):
    lowered = inputs.astype(jnp.bfloat16)
    return lax.optimization_barrier(lowered).astype(jnp.float32)

def one_sequence(q_in, k_in, v_in, g_in, gains):
    scale = 1.0 / math.sqrt(HD)
    q_unit, q_inv = unit_rows(q_in)
    k_unit, k_inv = unit_rows(k_in)
    q_gain = gains[0].reshape(HEADS, HD)
    k_gain = gains[1].reshape(HEADS, HD)
    q_norm = (q_unit * q_gain).reshape(SEQ, HEADS * HD).astype(jnp.bfloat16)
    k_norm = (k_unit * k_gain).reshape(SEQ, HEADS * HD).astype(jnp.bfloat16)
    padding = jnp.zeros((WINDOW, HEADS * HD), jnp.bfloat16)
    k_pad = jnp.concatenate([padding, k_norm], axis=0)
    v_pad = jnp.concatenate([padding, v_in], axis=0)
    rows = TOK_DEV
    span_cols = WINDOW + rows
    query_pos = lax.broadcasted_iota(jnp.int32, (rows, span_cols), 0)
    key_pos = lax.broadcasted_iota(jnp.int32, (rows, span_cols), 1)
    band = (key_pos > query_pos) & (key_pos <= query_pos + WINDOW)
    zero_grads = jnp.zeros((WINDOW + SEQ, HEADS * HD), jnp.float32)

    def step(carry, block):
        grad_k_pad, grad_v_pad = carry
        start = (block * rows).astype(jnp.int32)
        q_blk = lax.dynamic_slice_in_dim(q_norm, start, rows, 0).astype(jnp.float32).reshape(rows, HEADS, HD)
        g_blk = lax.dynamic_slice_in_dim(g_in, start, rows, 0).astype(jnp.float32).reshape(rows, HEADS, HD)
        k_blk = lax.dynamic_slice_in_dim(k_pad, start, span_cols, 0).astype(jnp.float32).reshape(span_cols, HEADS, HD)
        v_blk = lax.dynamic_slice_in_dim(v_pad, start, span_cols, 0).astype(jnp.float32).reshape(span_cols, HEADS, HD)
        visible = band & (key_pos + start >= WINDOW)
        scores = jnp.einsum('ahd,chd->hac', q_blk, k_blk) * scale
        total = lax.optimization_barrier(jnp.sum(jnp.where(visible, jnp.exp(scores), 0.0), axis=2, keepdims=True))
        probs = jnp.where(visible, jnp.exp(scores - jnp.log(total)), 0.0)
        probs_low = to_low(probs)
        attended = jnp.einsum('hac,chd->ahd', probs_low, v_blk)
        delta = jnp.transpose(lax.optimization_barrier(jnp.sum(g_blk * attended, axis=2)))[:, :, None]
        grad_probs = jnp.einsum('ahd,chd->hac', g_blk, v_blk)
        grad_scores = to_low(probs * (grad_probs - delta))
        grad_q = jnp.einsum('hac,chd->ahd', grad_scores, k_blk) * scale
        grad_k = jnp.einsum('hac,ahd->chd', grad_scores, q_blk) * scale
        grad_v = jnp.einsum('hac,ahd->chd', probs_low, g_blk)
        old_k = lax.dynamic_slice_in_dim(grad_k_pad, start, span_cols, 0)
        old_v = lax.dynamic_slice_in_dim(grad_v_pad, start, span_cols, 0)
        grad_k_pad = lax.dynamic_update_slice_in_dim(grad_k_pad, old_k + grad_k.reshape(span_cols, HEADS * HD), start, 0)
        grad_v_pad = lax.dynamic_update_slice_in_dim(grad_v_pad, old_v + grad_v.reshape(span_cols, HEADS * HD), start, 0)
        return ((grad_k_pad, grad_v_pad), grad_q.reshape(rows, HEADS * HD))
    blocks = jnp.arange(SEQ // rows, dtype=jnp.int32)
    (grad_k_pad, grad_v_pad), grad_q_blocks = lax.scan(step, (zero_grads, zero_grads), blocks)
    grad_qn = grad_q_blocks.reshape(SEQ, HEADS * HD)
    grad_queries, q_gain_grad = norm_backward(grad_qn, q_unit, q_inv, q_gain)
    grad_keys, k_gain_grad = norm_backward(grad_k_pad[WINDOW:], k_unit, k_inv, k_gain)
    grad_values = grad_v_pad[WINDOW:].astype(jnp.bfloat16)
    return (grad_queries, grad_keys, grad_values, jnp.stack([q_gain_grad, k_gain_grad]))

def reference(queries, keys, values, grad_out, gains):

    def per_sequence(items):
        return one_sequence(items[0], items[1], items[2], items[3], gains)
    grad_queries, grad_keys, grad_values, gain_parts = lax.map(per_sequence, (queries, keys, values, grad_out))
    return (grad_queries, grad_keys, grad_values, lax.optimization_barrier(jnp.sum(gain_parts, axis=0)))
```

```python
import functools
import math

import jax
import jax.numpy as jnp
from jax import lax
from jax.experimental import pallas as pl
from jax.experimental.pallas import tpu as pltpu
from jax.sharding import PartitionSpec as P

HEADS = 4
HD = 128
EPS = 1e-06
HALF = 256
SCALE = 1.0 / math.sqrt(HD)
EXP2_SCALE = SCALE * math.log2(math.e)
MESH = pl.DeviceIdType.MESH

OWN_BLOCKS = ((0, 0, True), (0, 1, False), (1, 1, True))
AHEAD_BLOCKS = ((0, 0, True), (1, 0, False), (1, 1, True))


def half(i):
    return pl.ds(i * HALF, HALF)


def dot_nt(a, b):
    return lax.dot_general(a, b, (((1,), (1,)), ((), ())), preferred_element_type=jnp.float32)


def dot(a, b):
    return jnp.dot(a, b, preferred_element_type=jnp.float32)


def unit_rows(x):
    wide = x.astype(jnp.float32)
    inverse = lax.rsqrt(jnp.mean(wide * wide, axis=1, keepdims=True) + EPS)
    return wide * inverse, inverse


def norm_back(grad, unit, inverse, gain):
    scaled = grad * gain
    mean_term = jnp.mean(scaled * unit, axis=1, keepdims=True)
    return (inverse * (scaled - unit * mean_term)).astype(jnp.bfloat16)


def exps_and_sums(h, blocks, own, kn, v, qn, g, qh, e, gp, eh, sums):
    total = [None, None]
    weighted = [None, None]
    for kb, qb, edge in blocks:
        s = dot_nt(kn[h, half(kb), :], qn[qh, half(qb), :])
        ex = jnp.exp2(s * EXP2_SCALE)
        if edge:
            key = lax.broadcasted_iota(jnp.int32, (HALF, HALF), 0)
            query = lax.broadcasted_iota(jnp.int32, (HALF, HALF), 1)
            ex = jnp.where(key <= query if own else key > query, ex, 0.0)
        gr = dot_nt(v[h, half(kb), :], g[h, half(qb), :])
        e[eh, half(kb), half(qb)] = ex
        gp[eh, half(kb), half(qb)] = gr
        t = jnp.sum(ex, axis=0, keepdims=True)
        w = jnp.sum(ex * gr, axis=0, keepdims=True)
        total[qb] = t if total[qb] is None else total[qb] + t
        weighted[qb] = w if weighted[qb] is None else weighted[qb] + w
    for qb in range(2):
        for i in range(2):
            sums[h, pl.ds(2 * qb + i, 1), :] = total[qb][:, i * HD : (i + 1) * HD]
            sums[h, pl.ds(4 + 2 * qb + i, 1), :] = weighted[qb][:, i * HD : (i + 1) * HD]


def row_pair(ref, h, first):
    return jnp.concatenate([ref[h, pl.ds(first, 1), :], ref[h, pl.ds(first + 1, 1), :]], axis=1)


def probs_and_grads(h, blocks, e, gp, eh, sums_a, sums_b, keep, p_low, ds_low):
    recip, delta = [], []
    for qb in range(2):
        r = 1.0 / (row_pair(sums_a, h, 2 * qb) + row_pair(sums_b, h, 2 * qb))
        delta.append((row_pair(sums_a, h, 4 + 2 * qb) + row_pair(sums_b, h, 4 + 2 * qb)) * r)
        recip.append(r if keep is None else r * keep)
    for kb, qb, _ in blocks:
        p = e[eh, half(kb), half(qb)] * recip[qb]
        p_low[half(kb), half(qb)] = p.astype(jnp.bfloat16)
        ds_low[half(kb), half(qb)] = (p * (gp[eh, half(kb), half(qb)] - delta[qb])).astype(jnp.bfloat16)


def kernel(
    n_dp, n_ctx,
    q_hbm, k_hbm, v_hbm, g_hbm, gains,
    dq_hbm, dk_hbm, dv_hbm, gain_out,
    q, k, v, g, rq, rg, qn, kn, kt, rqn,
    e_own, gp_own, e_ahead, gp_ahead, p_low, ds_low,
    dk_acc, dv_acc, dq_own, dq_give, dq_take, dq_o, dk_o, dv_o,
    own_sums, right_sums, ahead_sums, left_sums,
    gain_part, dp_terms, ctx_terms,
    load_sem, fwd_send, fwd_recv, own_send, own_recv, ahead_send, ahead_recv,
    dq_send, dq_recv, out_sem, dp_send, dp_recv, ctx_send, ctx_recv,
):
    me_d, me_c = lax.axis_index("dp"), lax.axis_index("ctx")
    left, right = lax.rem(me_c + n_ctx - 1, n_ctx), lax.rem(me_c + 1, n_ctx)
    width = HEADS * HD // n_dp
    has_ahead = jnp.where(me_c < n_ctx - 1, 1.0, 0.0).astype(jnp.float32)

    loads = ((q_hbm, q), (g_hbm, g), (k_hbm, k), (v_hbm, v))

    def load(a, h):
        src, dst = loads[a]
        return pltpu.make_async_copy(src.at[0, :, pl.ds(h * HD, HD)], dst.at[h], load_sem.at[a, h])

    for h in range(HEADS):
        for a in range(4):
            load(a, h).start()

    barrier = pltpu.get_barrier_semaphore()

    @pl.loop(1, n_dp)
    def _(i):
        pl.semaphore_signal(barrier, inc=1, device_id={"dp": lax.rem(me_d + i, n_dp)}, device_id_type=MESH)

    @pl.loop(1, n_ctx)
    def _(i):
        pl.semaphore_signal(barrier, inc=1, device_id={"ctx": lax.rem(me_c + i, n_ctx)}, device_id_type=MESH)

    pl.semaphore_wait(barrier, n_dp + n_ctx - 2)

    def to_left(src, dst, send, recv):
        return pltpu.make_async_remote_copy(src, dst, send, recv, device_id={"ctx": left}, device_id_type=MESH)

    def to_right(src, dst, send, recv):
        return pltpu.make_async_remote_copy(src, dst, send, recv, device_id={"ctx": right}, device_id_type=MESH)

    def send_q(h):
        return to_left(q.at[h], rq.at[h], fwd_send.at[0, h], fwd_recv.at[0, h])

    def send_g(h):
        return to_left(g.at[h], rg.at[h], fwd_send.at[1, h], fwd_recv.at[1, h])

    def send_own_sums(h):
        return to_left(own_sums.at[h], right_sums.at[h], own_send.at[h], own_recv.at[h])

    def send_ahead_sums(h):
        return to_right(ahead_sums.at[h], left_sums.at[h], ahead_send.at[h], ahead_recv.at[h])

    def send_dq(h):
        return to_right(dq_give.at[h], dq_take.at[h], dq_send.at[h], dq_recv.at[h])

    def store(a, h):
        src, dst = ((dq_o, dq_hbm), (dk_o, dk_hbm), (dv_o, dv_hbm))[a]
        cols = pl.ds(pl.multiple_of(h * HD, HD), HD)
        return pltpu.make_async_copy(src.at[h], dst.at[0, :, cols], out_sem.at[a, h])

    for h in range(HEADS):
        load(0, h).wait()
        load(1, h).wait()
        send_q(h).start()
        send_g(h).start()
    for h in range(HEADS):
        load(2, h).wait()
        load(3, h).wait()

    def gain_row(row, h):
        return gains[pl.ds(row, 1), pl.ds(pl.multiple_of(h * HD, HD), HD)]

    @pl.loop(0, HEADS)
    def _(h):
        for i in range(2):
            unit_q, _ = unit_rows(q[h, half(i), :])
            qn[h, half(i), :] = (unit_q * gain_row(0, h)).astype(jnp.bfloat16)
            unit_k, _ = unit_rows(k[h, half(i), :])
            normed = unit_k * gain_row(1, h)
            kn[h, half(i), :] = normed.astype(jnp.bfloat16)
            kt[h, :, half(i)] = normed.T.astype(jnp.bfloat16)
        exps_and_sums(h, OWN_BLOCKS, True, kn, v, qn, g, h, e_own, gp_own, h, own_sums)
        send_own_sums(h).start()

    def finish_dq(h):
        send_dq(h).wait_recv()
        for i in range(2):
            grad = dq_own[h, half(i), :] + dq_take[h, half(i), :].astype(jnp.float32)
            unit_q, inv_q = unit_rows(q[h, half(i), :])
            dq_o[h, half(i), :] = norm_back(grad, unit_q, inv_q, gain_row(0, h))
        store(0, h).start()

    @pl.loop(0, HEADS)
    def _(h):
        send_q(h).wait_recv()
        for i in range(2):
            unit_q, _ = unit_rows(rq[h, half(i), :])
            rqn[0, half(i), :] = (unit_q * gain_row(0, h)).astype(jnp.bfloat16)
        send_g(h).wait_recv()
        exps_and_sums(h, AHEAD_BLOCKS, False, kn, v, rqn, rg, 0, e_ahead, gp_ahead, 0, ahead_sums)
        ahead_sums[h] = ahead_sums[h] * has_ahead
        send_ahead_sums(h).start()
        send_own_sums(h).wait_recv()
        probs_and_grads(h, AHEAD_BLOCKS, e_ahead, gp_ahead, 0, right_sums, ahead_sums, has_ahead, p_low, ds_low)
        gain_q = jnp.zeros((1, HD), jnp.float32)
        for i in range(2):
            if i == 0:
                dqt = dot(kt[h], ds_low[:, half(0)])
            else:
                dqt = dot(kt[h, :, half(1)], ds_low[half(1), half(1)])
            grad = dqt.T * SCALE
            dq_give[h, half(i), :] = grad.astype(jnp.bfloat16)
            unit_q, _ = unit_rows(rq[h, half(i), :])
            gain_q += jnp.sum(grad * unit_q, axis=0, keepdims=True)
        send_dq(h).start()
        dk_acc[half(0), :] = dot(ds_low[half(0), half(0)], rqn[0, half(0), :])
        dk_acc[half(1), :] = dot(ds_low[half(1), :], rqn[0])
        dv_acc[half(0), :] = dot(p_low[half(0), half(0)], rg[h, half(0), :])
        dv_acc[half(1), :] = dot(p_low[half(1), :], rg[h])

        send_ahead_sums(h).wait_recv()
        probs_and_grads(h, OWN_BLOCKS, e_own, gp_own, h, own_sums, left_sums, None, p_low, ds_low)
        gain_k = jnp.zeros((1, HD), jnp.float32)
        for i in range(2):
            if i == 0:
                dk = dot(ds_low[half(0), :], qn[h])
                dv = dot(p_low[half(0), :], g[h])
                dqt = dot(kt[h, :, half(0)], ds_low[half(0), half(0)])
            else:
                dk = dot(ds_low[half(1), half(1)], qn[h, half(1), :])
                dv = dot(p_low[half(1), half(1)], g[h, half(1), :])
                dqt = dot(kt[h], ds_low[:, half(1)])
            dv_o[h, half(i), :] = (dv + dv_acc[half(i), :]).astype(jnp.bfloat16)
            grad_k = (dk + dk_acc[half(i), :]) * SCALE
            unit_k, inv_k = unit_rows(k[h, half(i), :])
            gain_k += jnp.sum(grad_k * unit_k, axis=0, keepdims=True)
            dk_o[h, half(i), :] = norm_back(grad_k, unit_k, inv_k, gain_row(1, h))
            grad_q = dqt.T * SCALE
            unit_q, _ = unit_rows(q[h, half(i), :])
            gain_q += jnp.sum(grad_q * unit_q, axis=0, keepdims=True)
            dq_own[h, half(i), :] = grad_q
        gain_part[h, pl.ds(0, 1), :] = gain_q
        gain_part[h, pl.ds(1, 1), :] = gain_k
        store(1, h).start()
        store(2, h).start()

        @pl.when(h > 0)
        def _():
            finish_dq(h - 1)

    def head_of(d):
        return lax.div(d * width, HD)

    def send_dp(i):
        to = lax.rem(me_d + i, n_dp)
        return pltpu.make_async_remote_copy(
            gain_part.at[head_of(to)], dp_terms.at[i], dp_send.at[i], dp_recv.at[i],
            device_id={"dp": to}, device_id_type=MESH,
        )

    def send_ctx(i):
        to = lax.rem(me_c + i, n_ctx)
        return pltpu.make_async_remote_copy(
            ctx_terms.at[me_c], ctx_terms.at[me_c], ctx_send.at[i], ctx_recv.at[i],
            device_id={"ctx": to}, device_id_type=MESH,
        )

    @pl.loop(1, n_dp)
    def _(i):
        send_dp(i).start()

    @pl.loop(1, n_dp)
    def _(i):
        send_dp(i).wait_recv()

    term = gain_part[head_of(me_d)]
    for i in range(1, n_dp):
        term = term + dp_terms[i]
    ctx_terms[me_c] = term

    @pl.loop(1, n_ctx)
    def _(i):
        send_ctx(i).start()

    finish_dq(HEADS - 1)

    def from_ctx(i):
        at = lax.rem(me_c + n_ctx - i, n_ctx)
        return pltpu.make_async_remote_copy(
            ctx_terms.at[at], ctx_terms.at[at], ctx_send.at[i], ctx_recv.at[i],
            device_id={"ctx": lax.rem(me_c + i, n_ctx)}, device_id_type=MESH,
        )

    @pl.loop(1, n_ctx)
    def _(i):
        from_ctx(i).wait_recv()

    total = ctx_terms[0]
    for i in range(1, n_ctx):
        total = total + ctx_terms[i]
    per_head = HD // width
    for j in range(per_head):

        @pl.when(lax.rem(me_d, per_head) == j)
        def _(j=j):
            gain_out[...] = total[:, j * width : (j + 1) * width]

    @pl.loop(0, HEADS)
    def _(h):
        send_q(h).wait_send()
        send_g(h).wait_send()
        send_own_sums(h).wait_send()
        send_ahead_sums(h).wait_send()
        send_dq(h).wait_send()
        for a in range(3):
            store(a, h).wait()

    @pl.loop(1, n_dp)
    def _(i):
        send_dp(i).wait_send()

    @pl.loop(1, n_ctx)
    def _(i):
        send_ctx(i).wait_send()


def per_device(n_dp, n_ctx, queries, keys, values, grad_out, gains):
    rows = queries.shape[1]
    low, wide = jnp.bfloat16, jnp.float32
    heads_low = pltpu.VMEM((HEADS, rows, HD), low)
    sums = pltpu.VMEM((HEADS, 8, HD), wide)
    dma = pltpu.SemaphoreType.DMA
    any_space = pl.BlockSpec(memory_space=pl.ANY)
    vmem = pl.BlockSpec(memory_space=pltpu.VMEM)
    big = jax.ShapeDtypeStruct(queries.shape, low)
    return pl.pallas_call(
        functools.partial(kernel, n_dp, n_ctx),
        out_shape=(big, big, big, jax.ShapeDtypeStruct((2, HEADS * HD // n_dp), wide)),
        in_specs=[any_space] * 4 + [vmem],
        out_specs=(any_space, any_space, any_space, vmem),
        scratch_shapes=[heads_low] * 8
        + [
            pltpu.VMEM((HEADS, HD, rows), low),
            pltpu.VMEM((1, rows, HD), low),
            pltpu.VMEM((HEADS, rows, rows), wide),
            pltpu.VMEM((HEADS, rows, rows), wide),
            pltpu.VMEM((1, rows, rows), wide),
            pltpu.VMEM((1, rows, rows), wide),
            pltpu.VMEM((rows, rows), low),
            pltpu.VMEM((rows, rows), low),
            pltpu.VMEM((rows, HD), wide),
            pltpu.VMEM((rows, HD), wide),
            pltpu.VMEM((HEADS, rows, HD), wide),
        ]
        + [heads_low] * 5
        + [sums] * 4
        + [
            pltpu.VMEM((HEADS, 2, HD), wide),
            pltpu.VMEM((n_dp, 2, HD), wide),
            pltpu.VMEM((n_ctx, 2, HD), wide),
            dma((4, HEADS)),
            dma((2, HEADS)),
            dma((2, HEADS)),
            dma((HEADS,)),
            dma((HEADS,)),
            dma((HEADS,)),
            dma((HEADS,)),
            dma((HEADS,)),
            dma((HEADS,)),
            dma((3, HEADS)),
            dma((n_dp,)),
            dma((n_dp,)),
            dma((n_ctx,)),
            dma((n_ctx,)),
        ],
        compiler_params=pltpu.CompilerParams(
            collective_id=0, has_side_effects=True, vmem_limit_bytes=48 * 1024 * 1024
        ),
    )(queries, keys, values, grad_out, gains)


def solution(mesh):
    placed = (
        P("dp", "ctx", None),
        P("dp", "ctx", None),
        P("dp", "ctx", None),
        P("dp", "ctx", None),
        P(),
    )
    return jax.shard_map(
        functools.partial(per_device, mesh.shape["dp"], mesh.shape["ctx"]),
        mesh=mesh,
        in_specs=placed,
        out_specs=(P("dp", "ctx", None), P("dp", "ctx", None), P("dp", "ctx", None), P(None, "dp")),
        check_vma=False,
    )
```

```python
import functools
import math

import jax
import jax.numpy as jnp
from jax import lax
from jax.experimental import pallas as pl
from jax.experimental.pallas import tpu as pltpu
from jax.sharding import PartitionSpec as P

HEADS = 4
HD = 128
EPS = 1e-06
HALF = 256
SCALE = 1.0 / math.sqrt(HD)
EXP2_SCALE = SCALE * math.log2(math.e)
MESH = pl.DeviceIdType.MESH

OWN_BLOCKS = ((0, 0, True), (0, 1, False), (1, 1, True))
AHEAD_BLOCKS = ((0, 0, True), (1, 0, False), (1, 1, True))


def half(i):
    return pl.ds(i * HALF, HALF)


def dot_nt(a, b):
    return lax.dot_general(a, b, (((1,), (1,)), ((), ())), preferred_element_type=jnp.float32)


def dot(a, b):
    return jnp.dot(a, b, preferred_element_type=jnp.float32)


def unit_rows(x):
    wide = x.astype(jnp.float32)
    inverse = lax.rsqrt(jnp.mean(wide * wide, axis=1, keepdims=True) + EPS)
    return wide * inverse, inverse


def norm_back(grad, unit, inverse, gain):
    scaled = grad * gain
    mean_term = jnp.mean(scaled * unit, axis=1, keepdims=True)
    return (inverse * (scaled - unit * mean_term)).astype(jnp.bfloat16)


def exps_and_sums(h, blocks, own, kn, v, qn, g, qh, e, gp, eh, sums):
    total = [None, None]
    weighted = [None, None]
    for kb, qb, edge in blocks:
        s = dot_nt(kn[h, half(kb), :], qn[qh, half(qb), :])
        ex = jnp.exp2(s * EXP2_SCALE)
        if edge:
            key = lax.broadcasted_iota(jnp.int32, (HALF, HALF), 0)
            query = lax.broadcasted_iota(jnp.int32, (HALF, HALF), 1)
            ex = jnp.where(key <= query if own else key > query, ex, 0.0)
        gr = dot_nt(v[h, half(kb), :], g[h, half(qb), :])
        e[eh, half(kb), half(qb)] = ex
        gp[eh, half(kb), half(qb)] = gr
        t = jnp.sum(ex, axis=0, keepdims=True)
        w = jnp.sum(ex * gr, axis=0, keepdims=True)
        total[qb] = t if total[qb] is None else total[qb] + t
        weighted[qb] = w if weighted[qb] is None else weighted[qb] + w
    for qb in range(2):
        for i in range(2):
            sums[h, pl.ds(2 * qb + i, 1), :] = total[qb][:, i * HD : (i + 1) * HD]
            sums[h, pl.ds(4 + 2 * qb + i, 1), :] = weighted[qb][:, i * HD : (i + 1) * HD]


def row_pair(ref, h, first):
    return jnp.concatenate([ref[h, pl.ds(first, 1), :], ref[h, pl.ds(first + 1, 1), :]], axis=1)


def probs_and_grads(h, blocks, e, gp, eh, sums_a, sums_b, keep, p_low, ds_low):
    recip, delta = [], []
    for qb in range(2):
        r = 1.0 / (row_pair(sums_a, h, 2 * qb) + row_pair(sums_b, h, 2 * qb))
        delta.append((row_pair(sums_a, h, 4 + 2 * qb) + row_pair(sums_b, h, 4 + 2 * qb)) * r)
        recip.append(r if keep is None else r * keep)
    for kb, qb, _ in blocks:
        p = e[eh, half(kb), half(qb)] * recip[qb]
        p_low[half(kb), half(qb)] = p.astype(jnp.bfloat16)
        ds_low[half(kb), half(qb)] = (p * (gp[eh, half(kb), half(qb)] - delta[qb])).astype(jnp.bfloat16)


def kernel(
    n_dp, n_ctx,
    q_hbm, k_hbm, v_hbm, g_hbm, gains,
    dq_hbm, dk_hbm, dv_hbm, gain_out,
    q, k, v, g, rq, rg, qn, kn, kt, rqn,
    e_own, gp_own, e_ahead, gp_ahead, p_low, ds_low,
    dk_acc, dv_acc, dq_own, dq_give, dq_take, dq_o, dk_o, dv_o,
    own_sums, right_sums, ahead_sums, left_sums,
    gain_part, dp_terms, ctx_terms,
    load_sem, fwd_send, fwd_recv, own_send, own_recv, ahead_send, ahead_recv,
    dq_send, dq_recv, out_sem, dp_send, dp_recv, ctx_send, ctx_recv,
):
    me_d, me_c = lax.axis_index("dp"), lax.axis_index("ctx")
    left, right = lax.rem(me_c + n_ctx - 1, n_ctx), lax.rem(me_c + 1, n_ctx)
    width = HEADS * HD // n_dp
    has_ahead = jnp.where(me_c < n_ctx - 1, 1.0, 0.0).astype(jnp.float32)

    loads = ((q_hbm, q), (g_hbm, g), (k_hbm, k), (v_hbm, v))

    def load(a, h):
        src, dst = loads[a]
        return pltpu.make_async_copy(src.at[0, :, pl.ds(h * HD, HD)], dst.at[h], load_sem.at[a, h])

    for h in range(HEADS):
        for a in range(4):
            load(a, h).start()

    barrier = pltpu.get_barrier_semaphore()

    @pl.loop(1, n_dp)
    def _(i):
        pl.semaphore_signal(barrier, inc=1, device_id={"dp": lax.rem(me_d + i, n_dp)}, device_id_type=MESH)

    @pl.loop(1, n_ctx)
    def _(i):
        pl.semaphore_signal(barrier, inc=1, device_id={"ctx": lax.rem(me_c + i, n_ctx)}, device_id_type=MESH)

    pl.semaphore_wait(barrier, n_dp + n_ctx - 2)

    def to_left(src, dst, send, recv):
        return pltpu.make_async_remote_copy(src, dst, send, recv, device_id={"ctx": left}, device_id_type=MESH)

    def to_right(src, dst, send, recv):
        return pltpu.make_async_remote_copy(src, dst, send, recv, device_id={"ctx": right}, device_id_type=MESH)

    def send_q(h):
        return to_left(q.at[h], rq.at[h], fwd_send.at[0, h], fwd_recv.at[0, h])

    def send_g(h):
        return to_left(g.at[h], rg.at[h], fwd_send.at[1, h], fwd_recv.at[1, h])

    def send_own_sums(h):
        return to_left(own_sums.at[h], right_sums.at[h], own_send.at[h], own_recv.at[h])

    def send_ahead_sums(h):
        return to_right(ahead_sums.at[h], left_sums.at[h], ahead_send.at[h], ahead_recv.at[h])

    def send_dq(h):
        return to_right(dq_give.at[h], dq_take.at[h], dq_send.at[h], dq_recv.at[h])

    def store(a, h):
        src, dst = ((dq_o, dq_hbm), (dk_o, dk_hbm), (dv_o, dv_hbm))[a]
        cols = pl.ds(pl.multiple_of(h * HD, HD), HD)
        return pltpu.make_async_copy(src.at[h], dst.at[0, :, cols], out_sem.at[a, h])

    def send_ahead(h):
        send_q(h).start()
        send_g(h).start()

    for h in range(HEADS):
        load(0, h).wait()
        load(1, h).wait()
        if h == 0:
            send_ahead(0)
    for h in range(HEADS):
        load(2, h).wait()
        load(3, h).wait()

    def gain_row(row, h):
        return gains[pl.ds(row, 1), pl.ds(pl.multiple_of(h * HD, HD), HD)]

    @pl.loop(0, HEADS)
    def _(h):
        for i in range(2):
            unit_q, _ = unit_rows(q[h, half(i), :])
            qn[h, half(i), :] = (unit_q * gain_row(0, h)).astype(jnp.bfloat16)
            unit_k, _ = unit_rows(k[h, half(i), :])
            normed = unit_k * gain_row(1, h)
            kn[h, half(i), :] = normed.astype(jnp.bfloat16)
            kt[h, :, half(i)] = normed.T.astype(jnp.bfloat16)
        exps_and_sums(h, OWN_BLOCKS, True, kn, v, qn, g, h, e_own, gp_own, h, own_sums)
        send_own_sums(h).start()

        @pl.when(h == 1)
        def _():
            send_ahead(1)

    send_ahead(2)
    send_ahead(3)

    def finish_dq(h):
        send_dq(h).wait_recv()
        for i in range(2):
            grad = dq_own[h, half(i), :] + dq_take[h, half(i), :].astype(jnp.float32)
            unit_q, inv_q = unit_rows(q[h, half(i), :])
            dq_o[h, half(i), :] = norm_back(grad, unit_q, inv_q, gain_row(0, h))
        store(0, h).start()

    @pl.loop(0, HEADS)
    def _(h):
        send_q(h).wait_recv()
        for i in range(2):
            unit_q, _ = unit_rows(rq[h, half(i), :])
            rqn[0, half(i), :] = (unit_q * gain_row(0, h)).astype(jnp.bfloat16)
        send_g(h).wait_recv()

        @pl.when(h == HEADS - 1)
        def _():
            send_dq(0).start()

        exps_and_sums(h, AHEAD_BLOCKS, False, kn, v, rqn, rg, 0, e_ahead, gp_ahead, 0, ahead_sums)
        ahead_sums[h] = ahead_sums[h] * has_ahead
        send_ahead_sums(h).start()
        send_own_sums(h).wait_recv()
        probs_and_grads(h, AHEAD_BLOCKS, e_ahead, gp_ahead, 0, right_sums, ahead_sums, has_ahead, p_low, ds_low)
        gain_q = jnp.zeros((1, HD), jnp.float32)
        for i in range(2):
            if i == 0:
                dqt = dot(kt[h], ds_low[:, half(0)])
            else:
                dqt = dot(kt[h, :, half(1)], ds_low[half(1), half(1)])
            grad = dqt.T * SCALE
            dq_give[h, half(i), :] = grad.astype(jnp.bfloat16)
            unit_q, _ = unit_rows(rq[h, half(i), :])
            gain_q += jnp.sum(grad * unit_q, axis=0, keepdims=True)
        gain_part[h, pl.ds(0, 1), :] = gain_q
        dk_acc[h, half(0), :] = dot(ds_low[half(0), half(0)], rqn[0, half(0), :])
        dk_acc[h, half(1), :] = dot(ds_low[half(1), :], rqn[0])
        dv_acc[h, half(0), :] = dot(p_low[half(0), half(0)], rg[h, half(0), :])
        dv_acc[h, half(1), :] = dot(p_low[half(1), :], rg[h])

    send_dq(1).start()

    @pl.loop(0, HEADS)
    def _(h):
        send_ahead_sums(h).wait_recv()
        probs_and_grads(h, OWN_BLOCKS, e_own, gp_own, h, own_sums, left_sums, None, p_low, ds_low)
        gain_q = gain_part[h, pl.ds(0, 1), :]
        gain_k = jnp.zeros((1, HD), jnp.float32)
        for i in range(2):
            if i == 0:
                dk = dot(ds_low[half(0), :], qn[h])
                dv = dot(p_low[half(0), :], g[h])
                dqt = dot(kt[h, :, half(0)], ds_low[half(0), half(0)])
            else:
                dk = dot(ds_low[half(1), half(1)], qn[h, half(1), :])
                dv = dot(p_low[half(1), half(1)], g[h, half(1), :])
                dqt = dot(kt[h], ds_low[:, half(1)])
            dv_o[h, half(i), :] = (dv + dv_acc[h, half(i), :]).astype(jnp.bfloat16)
            grad_k = (dk + dk_acc[h, half(i), :]) * SCALE
            unit_k, inv_k = unit_rows(k[h, half(i), :])
            gain_k += jnp.sum(grad_k * unit_k, axis=0, keepdims=True)
            dk_o[h, half(i), :] = norm_back(grad_k, unit_k, inv_k, gain_row(1, h))
            grad_q = dqt.T * SCALE
            unit_q, _ = unit_rows(q[h, half(i), :])
            gain_q += jnp.sum(grad_q * unit_q, axis=0, keepdims=True)
            dq_own[h, half(i), :] = grad_q
        gain_part[h, pl.ds(0, 1), :] = gain_q
        gain_part[h, pl.ds(1, 1), :] = gain_k
        store(1, h).start()
        store(2, h).start()

    def head_of(d):
        return lax.div(d * width, HD)

    def send_dp(i):
        to = lax.rem(me_d + i, n_dp)
        return pltpu.make_async_remote_copy(
            gain_part.at[head_of(to)], dp_terms.at[i], dp_send.at[i], dp_recv.at[i],
            device_id={"dp": to}, device_id_type=MESH,
        )

    def send_ctx(i):
        to = lax.rem(me_c + i, n_ctx)
        return pltpu.make_async_remote_copy(
            ctx_terms.at[me_c], ctx_terms.at[me_c], ctx_send.at[i], ctx_recv.at[i],
            device_id={"ctx": to}, device_id_type=MESH,
        )

    @pl.loop(1, n_dp)
    def _(i):
        send_dp(i).start()

    send_dq(2).start()
    send_dq(3).start()

    @pl.loop(1, n_dp)
    def _(i):
        send_dp(i).wait_recv()

    term = gain_part[head_of(me_d)]
    for i in range(1, n_dp):
        term = term + dp_terms[i]
    ctx_terms[me_c] = term

    @pl.loop(1, n_ctx)
    def _(i):
        send_ctx(i).start()

    @pl.loop(0, HEADS)
    def _(h):
        finish_dq(h)

    def from_ctx(i):
        at = lax.rem(me_c + n_ctx - i, n_ctx)
        return pltpu.make_async_remote_copy(
            ctx_terms.at[at], ctx_terms.at[at], ctx_send.at[i], ctx_recv.at[i],
            device_id={"ctx": lax.rem(me_c + i, n_ctx)}, device_id_type=MESH,
        )

    @pl.loop(1, n_ctx)
    def _(i):
        from_ctx(i).wait_recv()

    total = ctx_terms[0]
    for i in range(1, n_ctx):
        total = total + ctx_terms[i]
    per_head = HD // width
    for j in range(per_head):

        @pl.when(lax.rem(me_d, per_head) == j)
        def _(j=j):
            gain_out[...] = total[:, j * width : (j + 1) * width]

    @pl.loop(0, HEADS)
    def _(h):
        send_q(h).wait_send()
        send_g(h).wait_send()
        send_own_sums(h).wait_send()
        send_ahead_sums(h).wait_send()
        send_dq(h).wait_send()
        for a in range(3):
            store(a, h).wait()

    @pl.loop(1, n_dp)
    def _(i):
        send_dp(i).wait_send()

    @pl.loop(1, n_ctx)
    def _(i):
        send_ctx(i).wait_send()


def hand_out(*refs):
    sem = refs[8]
    copies = [pltpu.make_async_copy(refs[i], refs[4 + i], sem.at[i]) for i in range(4)]
    for copy in copies:
        copy.start()
    for copy in copies:
        copy.wait()


def per_device(n_dp, n_ctx, queries, keys, values, grad_out, gains):
    rows = queries.shape[1]
    low, wide = jnp.bfloat16, jnp.float32
    heads_low = pltpu.VMEM((HEADS, rows, HD), low)
    sums = pltpu.VMEM((HEADS, 8, HD), wide)
    dma = pltpu.SemaphoreType.DMA
    any_space = pl.BlockSpec(memory_space=pl.ANY)
    vmem = pl.BlockSpec(memory_space=pltpu.VMEM)
    big = pltpu.VMEM(queries.shape, low)
    hbm = pl.BlockSpec(memory_space=pltpu.HBM)
    results = pl.pallas_call(
        functools.partial(kernel, n_dp, n_ctx),
        out_shape=(big, big, big, pltpu.VMEM((2, HEADS * HD // n_dp), wide)),
        in_specs=[any_space] * 4 + [vmem],
        out_specs=(vmem,) * 4,
        scratch_shapes=[heads_low] * 8
        + [
            pltpu.VMEM((HEADS, HD, rows), low),
            pltpu.VMEM((1, rows, HD), low),
            pltpu.VMEM((HEADS, rows, rows), wide),
            pltpu.VMEM((HEADS, rows, rows), wide),
            pltpu.VMEM((1, rows, rows), wide),
            pltpu.VMEM((1, rows, rows), wide),
            pltpu.VMEM((rows, rows), low),
            pltpu.VMEM((rows, rows), low),
            pltpu.VMEM((HEADS, rows, HD), wide),
            pltpu.VMEM((HEADS, rows, HD), wide),
            pltpu.VMEM((HEADS, rows, HD), wide),
        ]
        + [heads_low] * 5
        + [sums] * 4
        + [
            pltpu.VMEM((HEADS, 2, HD), wide),
            pltpu.VMEM((n_dp, 2, HD), wide),
            pltpu.VMEM((n_ctx, 2, HD), wide),
            dma((4, HEADS)),
            dma((2, HEADS)),
            dma((2, HEADS)),
            dma((HEADS,)),
            dma((HEADS,)),
            dma((HEADS,)),
            dma((HEADS,)),
            dma((HEADS,)),
            dma((HEADS,)),
            dma((3, HEADS)),
            dma((n_dp,)),
            dma((n_dp,)),
            dma((n_ctx,)),
            dma((n_ctx,)),
        ],
        compiler_params=pltpu.CompilerParams(
            collective_id=0, has_side_effects=True, vmem_limit_bytes=60 * 1024 * 1024
        ),
    )(queries, keys, values, grad_out, gains)
    return pl.pallas_call(
        hand_out,
        out_shape=tuple(jax.ShapeDtypeStruct(r.shape, r.dtype) for r in results),
        in_specs=[any_space] * 4,
        out_specs=(hbm,) * 4,
        scratch_shapes=[dma((4,))],
        compiler_params=pltpu.CompilerParams(vmem_limit_bytes=2 * 1024 * 1024),
    )(*results)


def solution(mesh):
    placed = (
        P("dp", "ctx", None),
        P("dp", "ctx", None),
        P("dp", "ctx", None),
        P("dp", "ctx", None),
        P(),
    )
    return jax.shard_map(
        functools.partial(per_device, mesh.shape["dp"], mesh.shape["ctx"]),
        mesh=mesh,
        in_specs=placed,
        out_specs=(P("dp", "ctx", None), P("dp", "ctx", None), P("dp", "ctx", None), P(None, "dp")),
        check_vma=False,
    )
```

```python
import functools
import math

import jax
import jax.numpy as jnp
from jax import lax
from jax.experimental import pallas as pl
from jax.experimental.pallas import tpu as pltpu
from jax.sharding import PartitionSpec as P

HEADS = 4
HD = 128
EPS = 1e-06
HALF = 256
Z_HI, Z_LO = 2, 4
SCALE = 1.0 / math.sqrt(HD)
EXP2_SCALE = SCALE * math.log2(math.e)
MESH = pl.DeviceIdType.MESH

OWN_BLOCKS = ((0, 0, True), (0, 1, False), (1, 1, True))
AHEAD_BLOCKS = ((0, 0, True), (1, 0, False), (1, 1, True))


def half(i):
    return pl.ds(i * HALF, HALF)


def dot_nt(a, b):
    return lax.dot_general(a, b, (((1,), (1,)), ((), ())), preferred_element_type=jnp.float32)


def dot(a, b):
    return jnp.dot(a, b, preferred_element_type=jnp.float32)


def unit_rows(x):
    wide = x.astype(jnp.float32)
    inverse = lax.rsqrt(jnp.mean(wide * wide, axis=1, keepdims=True) + EPS)
    return wide * inverse, inverse


def norm_back(grad, unit, inverse, gain):
    scaled = grad * gain
    mean_term = jnp.mean(scaled * unit, axis=1, keepdims=True)
    return (inverse * (scaled - unit * mean_term)).astype(jnp.bfloat16)


def exps_and_sums(h, blocks, own, kn, v, qn, g, qh, e, gp, eh, sums):
    total = [None, None]
    weighted = [None, None]
    for kb, qb, edge in blocks:
        s = dot_nt(kn[h, half(kb), :], qn[qh, half(qb), :])
        ex = jnp.exp2(s * EXP2_SCALE)
        if edge:
            key = lax.broadcasted_iota(jnp.int32, (HALF, HALF), 0)
            query = lax.broadcasted_iota(jnp.int32, (HALF, HALF), 1)
            ex = jnp.where(key <= query if own else key > query, ex, 0.0)
        gr = dot_nt(v[h, half(kb), :], g[h, half(qb), :])
        e[eh, half(kb), half(qb)] = ex
        gp[eh, half(kb), half(qb)] = gr
        t = jnp.sum(ex, axis=0, keepdims=True)
        w = jnp.sum(ex * gr, axis=0, keepdims=True)
        total[qb] = t if total[qb] is None else total[qb] + t
        weighted[qb] = w if weighted[qb] is None else weighted[qb] + w
    for qb in range(2):
        for i in range(2):
            sums[h, pl.ds(2 * qb + i, 1), :] = total[qb][:, i * HD : (i + 1) * HD]
            sums[h, pl.ds(4 + 2 * qb + i, 1), :] = weighted[qb][:, i * HD : (i + 1) * HD]


def row_pair(ref, h, first):
    return jnp.concatenate([ref[h, pl.ds(first, 1), :], ref[h, pl.ds(first + 1, 1), :]], axis=1)


def probs_and_grads(h, blocks, e, gp, eh, sums_a, sums_b, keep, p_low, ds_low):
    recip, delta = [], []
    for qb in range(2):
        r = 1.0 / (row_pair(sums_a, h, 2 * qb) + row_pair(sums_b, h, 2 * qb))
        delta.append((row_pair(sums_a, h, 4 + 2 * qb) + row_pair(sums_b, h, 4 + 2 * qb)) * r)
        recip.append(r if keep is None else r * keep)
    for kb, qb, _ in blocks:
        p = e[eh, half(kb), half(qb)] * recip[qb]
        p_low[half(kb), half(qb)] = p.astype(jnp.bfloat16)
        ds_low[half(kb), half(qb)] = (p * (gp[eh, half(kb), half(qb)] - delta[qb])).astype(jnp.bfloat16)


def kernel(
    n_dp, n_ctx,
    q_hbm, k_hbm, v_hbm, g_hbm, gains,
    dq_hbm, dk_hbm, dv_hbm, gain_out,
    q, k, v, g, rq, rg, qn, kn, kt, rqn,
    e_own, gp_own, e_ahead, gp_ahead, p_low, ds_low,
    dk_acc, dv_acc, dq_own, dq_give, dq_take, dq_o, dk_o, dv_o,
    own_sums, right_sums, ahead_sums, left_sums,
    gain_part, gain_terms,
    load_sem, fwd_send, fwd_recv, own_send, own_recv, ahead_send, ahead_recv,
    dq_send, dq_recv, out_sem, gain_send, gain_recv,
):
    me_d, me_c = lax.axis_index("dp"), lax.axis_index("ctx")
    left, right = lax.rem(me_c + n_ctx - 1, n_ctx), lax.rem(me_c + 1, n_ctx)
    width = HEADS * HD // n_dp
    has_ahead = jnp.where(me_c < n_ctx - 1, 1.0, 0.0).astype(jnp.float32)

    loads = ((q_hbm, q), (g_hbm, g), (k_hbm, k), (v_hbm, v))

    def load(a, h):
        src, dst = loads[a]
        return pltpu.make_async_copy(src.at[0, :, pl.ds(h * HD, HD)], dst.at[h], load_sem.at[a, h])

    for h in range(HEADS):
        for a in range(4):
            load(a, h).start()

    barrier = pltpu.get_barrier_semaphore()

    n_in, n_y, n_z = n_dp // Z_HI, n_ctx // Z_LO, Z_HI * Z_LO
    me_in, me_y = lax.rem(me_d, n_in), lax.div(me_c, Z_LO)
    me_z = lax.div(me_d, n_in) * Z_LO + lax.rem(me_c, Z_LO)

    def device(axis, at):
        if axis == 0:
            return {"dp": me_d - me_in + at}
        if axis == 1:
            return {"ctx": lax.rem(me_c, Z_LO) + at * Z_LO}
        return {"dp": lax.div(at, Z_LO) * n_in + me_in, "ctx": me_y * Z_LO + lax.rem(at, Z_LO)}

    axes = ((n_in, me_in), (n_y, me_y), (n_z, me_z))

    for axis, (count, me) in enumerate(axes):

        @pl.loop(1, count)
        def _(i, axis=axis, count=count, me=me):
            pl.semaphore_signal(
                barrier, inc=1, device_id=device(axis, lax.rem(me + i, count)), device_id_type=MESH
            )

    for neighbour in (left, right):
        pl.semaphore_signal(barrier, inc=1, device_id={"ctx": neighbour}, device_id_type=MESH)
    pl.semaphore_wait(barrier, n_in + n_y + n_z - 1)

    def to_left(src, dst, send, recv):
        return pltpu.make_async_remote_copy(src, dst, send, recv, device_id={"ctx": left}, device_id_type=MESH)

    def to_right(src, dst, send, recv):
        return pltpu.make_async_remote_copy(src, dst, send, recv, device_id={"ctx": right}, device_id_type=MESH)

    def send_q(h):
        return to_left(q.at[h], rq.at[h], fwd_send.at[0, h], fwd_recv.at[0, h])

    def send_g(h):
        return to_left(g.at[h], rg.at[h], fwd_send.at[1, h], fwd_recv.at[1, h])

    def send_own_sums(h):
        return to_left(own_sums.at[h], right_sums.at[h], own_send.at[h], own_recv.at[h])

    def send_ahead_sums(h):
        return to_right(ahead_sums.at[h], left_sums.at[h], ahead_send.at[h], ahead_recv.at[h])

    def send_dq(h):
        return to_right(dq_give.at[h], dq_take.at[h], dq_send.at[h], dq_recv.at[h])

    def store(a, h):
        src, dst = ((dq_o, dq_hbm), (dk_o, dk_hbm), (dv_o, dv_hbm))[a]
        cols = pl.ds(pl.multiple_of(h * HD, HD), HD)
        return pltpu.make_async_copy(src.at[h], dst.at[0, :, cols], out_sem.at[a, h])

    def send_ahead(h):
        send_q(h).start()
        send_g(h).start()

    for h in range(HEADS):
        load(0, h).wait()
        load(1, h).wait()
        if h == 0:
            send_ahead(0)
    for h in range(HEADS):
        load(2, h).wait()
        load(3, h).wait()

    def gain_row(row, h):
        return gains[pl.ds(row, 1), pl.ds(pl.multiple_of(h * HD, HD), HD)]

    @pl.loop(0, HEADS)
    def _(h):
        for i in range(2):
            unit_q, _ = unit_rows(q[h, half(i), :])
            qn[h, half(i), :] = (unit_q * gain_row(0, h)).astype(jnp.bfloat16)
            unit_k, _ = unit_rows(k[h, half(i), :])
            normed = unit_k * gain_row(1, h)
            kn[h, half(i), :] = normed.astype(jnp.bfloat16)
            kt[h, :, half(i)] = normed.T.astype(jnp.bfloat16)
        exps_and_sums(h, OWN_BLOCKS, True, kn, v, qn, g, h, e_own, gp_own, h, own_sums)
        send_own_sums(h).start()

        @pl.when(h == 1)
        def _():
            send_ahead(1)

    send_ahead(2)
    send_ahead(3)

    def finish_dq(h):
        send_dq(h).wait_recv()
        for i in range(2):
            grad = dq_own[h, half(i), :] + dq_take[h, half(i), :].astype(jnp.float32)
            unit_q, inv_q = unit_rows(q[h, half(i), :])
            dq_o[h, half(i), :] = norm_back(grad, unit_q, inv_q, gain_row(0, h))
        store(0, h).start()

    @pl.loop(0, HEADS)
    def _(h):
        send_q(h).wait_recv()
        for i in range(2):
            unit_q, _ = unit_rows(rq[h, half(i), :])
            rqn[0, half(i), :] = (unit_q * gain_row(0, h)).astype(jnp.bfloat16)
        send_g(h).wait_recv()

        exps_and_sums(h, AHEAD_BLOCKS, False, kn, v, rqn, rg, 0, e_ahead, gp_ahead, 0, ahead_sums)
        ahead_sums[h] = ahead_sums[h] * has_ahead
        send_ahead_sums(h).start()

        @pl.when(h == HEADS - 1)
        def _():
            for earlier in range(HEADS - 1):
                send_dq(earlier).start()

        send_own_sums(h).wait_recv()
        probs_and_grads(h, AHEAD_BLOCKS, e_ahead, gp_ahead, 0, right_sums, ahead_sums, has_ahead, p_low, ds_low)
        gain_q = jnp.zeros((1, HD), jnp.float32)
        for i in range(2):
            if i == 0:
                dqt = dot(kt[h], ds_low[:, half(0)])
            else:
                dqt = dot(kt[h, :, half(1)], ds_low[half(1), half(1)])
            grad = dqt.T * SCALE
            dq_give[h, half(i), :] = grad.astype(jnp.bfloat16)
            unit_q, _ = unit_rows(rq[h, half(i), :])
            gain_q += jnp.sum(grad * unit_q, axis=0, keepdims=True)

        @pl.when(h == HEADS - 1)
        def _():
            send_dq(HEADS - 1).start()

        gain_part[0, h, pl.ds(0, 1), :] = gain_q
        dk_acc[h, half(0), :] = dot(ds_low[half(0), half(0)], rqn[0, half(0), :])
        dk_acc[h, half(1), :] = dot(ds_low[half(1), :], rqn[0])
        dv_acc[h, half(0), :] = dot(p_low[half(0), half(0)], rg[h, half(0), :])
        dv_acc[h, half(1), :] = dot(p_low[half(1), :], rg[h])

    @pl.loop(0, HEADS)
    def _(h):
        send_ahead_sums(h).wait_recv()
        probs_and_grads(h, OWN_BLOCKS, e_own, gp_own, h, own_sums, left_sums, None, p_low, ds_low)
        gain_q = gain_part[0, h, pl.ds(0, 1), :]
        gain_k = jnp.zeros((1, HD), jnp.float32)
        for i in range(2):
            if i == 0:
                dk = dot(ds_low[half(0), :], qn[h])
                dv = dot(p_low[half(0), :], g[h])
                dqt = dot(kt[h, :, half(0)], ds_low[half(0), half(0)])
            else:
                dk = dot(ds_low[half(1), half(1)], qn[h, half(1), :])
                dv = dot(p_low[half(1), half(1)], g[h, half(1), :])
                dqt = dot(kt[h], ds_low[:, half(1)])
            dv_o[h, half(i), :] = (dv + dv_acc[h, half(i), :]).astype(jnp.bfloat16)
            grad_k = (dk + dk_acc[h, half(i), :]) * SCALE
            unit_k, inv_k = unit_rows(k[h, half(i), :])
            gain_k += jnp.sum(grad_k * unit_k, axis=0, keepdims=True)
            dk_o[h, half(i), :] = norm_back(grad_k, unit_k, inv_k, gain_row(1, h))
            grad_q = dqt.T * SCALE
            unit_q, _ = unit_rows(q[h, half(i), :])
            gain_q += jnp.sum(grad_q * unit_q, axis=0, keepdims=True)
            dq_own[h, half(i), :] = grad_q
        gain_part[0, h, pl.ds(0, 1), :] = gain_q
        gain_part[0, h, pl.ds(1, 1), :] = gain_k
        store(1, h).start()
        store(2, h).start()

    def send_gain(axis, i):
        count, me = axes[axis]
        return pltpu.make_async_remote_copy(
            gain_part.at[axis], gain_terms.at[axis, me], gain_send.at[axis, i], gain_recv.at[axis, i],
            device_id=device(axis, lax.rem(me + i, count)), device_id_type=MESH,
        )

    def start_gains(axis):
        @pl.loop(1, axes[axis][0])
        def _(i):
            send_gain(axis, i).start()

    def sum_gains(axis):
        count, me = axes[axis]
        gain_terms[axis, me] = gain_part[axis]

        @pl.loop(1, count)
        def _(i):
            at = gain_terms.at[axis, lax.rem(me + count - i, count)]
            pltpu.make_async_remote_copy(
                at, at, gain_send.at[axis, i], gain_recv.at[axis, i],
                device_id=device(axis, lax.rem(me + i, count)), device_id_type=MESH,
            ).wait_recv()

        total = gain_terms[axis, 0]
        for i in range(1, count):
            total = total + gain_terms[axis, i]
        gain_part[axis + 1] = total

    start_gains(0)
    sum_gains(0)
    start_gains(1)
    sum_gains(1)
    start_gains(2)

    @pl.loop(0, HEADS)
    def _(h):
        finish_dq(h)

    sum_gains(2)
    per_head = HD // width
    mine = gain_part[3, lax.div(me_d, per_head)]
    for j in range(per_head):

        @pl.when(lax.rem(me_d, per_head) == j)
        def _(j=j):
            gain_out[...] = mine[:, j * width : (j + 1) * width]

    @pl.loop(0, HEADS)
    def _(h):
        send_q(h).wait_send()
        send_g(h).wait_send()
        send_own_sums(h).wait_send()
        send_ahead_sums(h).wait_send()
        send_dq(h).wait_send()
        for a in range(3):
            store(a, h).wait()

    for axis in range(3):

        @pl.loop(1, axes[axis][0])
        def _(i, axis=axis):
            send_gain(axis, i).wait_send()


def hand_out(*refs):
    sem = refs[8]
    copies = [pltpu.make_async_copy(refs[i], refs[4 + i], sem.at[i]) for i in range(4)]
    for copy in copies:
        copy.start()
    for copy in copies:
        copy.wait()


def per_device(n_dp, n_ctx, queries, keys, values, grad_out, gains):
    rows = queries.shape[1]
    most = max(n_dp // Z_HI, n_ctx // Z_LO, Z_HI * Z_LO)
    low, wide = jnp.bfloat16, jnp.float32
    heads_low = pltpu.VMEM((HEADS, rows, HD), low)
    sums = pltpu.VMEM((HEADS, 8, HD), wide)
    dma = pltpu.SemaphoreType.DMA
    any_space = pl.BlockSpec(memory_space=pl.ANY)
    vmem = pl.BlockSpec(memory_space=pltpu.VMEM)
    big = pltpu.VMEM(queries.shape, low)
    hbm = pl.BlockSpec(memory_space=pltpu.HBM)
    results = pl.pallas_call(
        functools.partial(kernel, n_dp, n_ctx),
        out_shape=(big, big, big, pltpu.VMEM((2, HEADS * HD // n_dp), wide)),
        in_specs=[any_space] * 4 + [vmem],
        out_specs=(vmem,) * 4,
        scratch_shapes=[heads_low] * 8
        + [
            pltpu.VMEM((HEADS, HD, rows), low),
            pltpu.VMEM((1, rows, HD), low),
            pltpu.VMEM((HEADS, rows, rows), wide),
            pltpu.VMEM((HEADS, rows, rows), wide),
            pltpu.VMEM((1, rows, rows), wide),
            pltpu.VMEM((1, rows, rows), wide),
            pltpu.VMEM((rows, rows), low),
            pltpu.VMEM((rows, rows), low),
            pltpu.VMEM((HEADS, rows, HD), wide),
            pltpu.VMEM((HEADS, rows, HD), wide),
            pltpu.VMEM((HEADS, rows, HD), wide),
        ]
        + [heads_low] * 5
        + [sums] * 4
        + [
            pltpu.VMEM((4, HEADS, 2, HD), wide),
            pltpu.VMEM((3, most, HEADS, 2, HD), wide),
            dma((4, HEADS)),
            dma((2, HEADS)),
            dma((2, HEADS)),
            dma((HEADS,)),
            dma((HEADS,)),
            dma((HEADS,)),
            dma((HEADS,)),
            dma((HEADS,)),
            dma((HEADS,)),
            dma((3, HEADS)),
            dma((3, most)),
            dma((3, most)),
        ],
        compiler_params=pltpu.CompilerParams(
            collective_id=0, has_side_effects=True, vmem_limit_bytes=60 * 1024 * 1024
        ),
    )(queries, keys, values, grad_out, gains)
    return pl.pallas_call(
        hand_out,
        out_shape=tuple(jax.ShapeDtypeStruct(r.shape, r.dtype) for r in results),
        in_specs=[any_space] * 4,
        out_specs=(hbm,) * 4,
        scratch_shapes=[dma((4,))],
        compiler_params=pltpu.CompilerParams(vmem_limit_bytes=2 * 1024 * 1024),
    )(*results)


def solution(mesh):
    placed = (
        P("dp", "ctx", None),
        P("dp", "ctx", None),
        P("dp", "ctx", None),
        P("dp", "ctx", None),
        P(),
    )
    return jax.shard_map(
        functools.partial(per_device, mesh.shape["dp"], mesh.shape["ctx"]),
        mesh=mesh,
        in_specs=placed,
        out_specs=(P("dp", "ctx", None), P("dp", "ctx", None), P("dp", "ctx", None), P(None, "dp")),
        check_vma=False,
    )
```

```python
import functools
import math

import jax
import jax.numpy as jnp
from jax import lax
from jax.experimental import pallas as pl
from jax.experimental.pallas import tpu as pltpu
from jax.sharding import PartitionSpec as P

HEADS = 4
HD = 128
EPS = 1e-06
HALF = 256
LAST = HEADS - 1
Z_HI, Z_LO = 2, 4
SCALE = 1.0 / math.sqrt(HD)
EXP2_SCALE = SCALE * math.log2(math.e)
MESH = pl.DeviceIdType.MESH

OWN_BLOCKS = ((0, 0, True), (0, 1, False), (1, 1, True))
AHEAD_BLOCKS = ((0, 0, True), (1, 0, False), (1, 1, True))


def half(i):
    return pl.ds(i * HALF, HALF)


def dot_nt(a, b):
    return lax.dot_general(a, b, (((1,), (1,)), ((), ())), preferred_element_type=jnp.float32)


def dot(a, b):
    return jnp.dot(a, b, preferred_element_type=jnp.float32)


def unit_rows(x):
    wide = x.astype(jnp.float32)
    inverse = lax.rsqrt(jnp.mean(wide * wide, axis=1, keepdims=True) + EPS)
    return wide * inverse, inverse


def norm_back(grad, unit, inverse, gain):
    scaled = grad * gain
    mean_term = jnp.mean(scaled * unit, axis=1, keepdims=True)
    return (inverse * (scaled - unit * mean_term)).astype(jnp.bfloat16)


def exps_and_sums(h, blocks, own, kn, kh, v, qn, qh, g, e, gp, eh, sums):
    total = [None, None]
    weighted = [None, None]
    for kb, qb, edge in blocks:
        s = dot_nt(kn[kh, half(kb), :], qn[qh, half(qb), :])
        ex = jnp.exp2(s * EXP2_SCALE)
        if edge:
            key = lax.broadcasted_iota(jnp.int32, (HALF, HALF), 0)
            query = lax.broadcasted_iota(jnp.int32, (HALF, HALF), 1)
            ex = jnp.where(key <= query if own else key > query, ex, 0.0)
        gr = dot_nt(v[h, half(kb), :], g[h, half(qb), :])
        e[eh, half(kb), half(qb)] = ex
        gp[eh, half(kb), half(qb)] = gr
        t = jnp.sum(ex, axis=0, keepdims=True)
        w = jnp.sum(ex * gr, axis=0, keepdims=True)
        total[qb] = t if total[qb] is None else total[qb] + t
        weighted[qb] = w if weighted[qb] is None else weighted[qb] + w
    for qb in range(2):
        for i in range(2):
            sums[h, pl.ds(2 * qb + i, 1), :] = total[qb][:, i * HD : (i + 1) * HD]
            sums[h, pl.ds(4 + 2 * qb + i, 1), :] = weighted[qb][:, i * HD : (i + 1) * HD]


def row_pair(ref, h, first):
    return jnp.concatenate([ref[h, pl.ds(first, 1), :], ref[h, pl.ds(first + 1, 1), :]], axis=1)


def probs_and_grads(h, blocks, e, gp, eh, sums_a, sums_b, keep, p_low, ds_low):
    recip, delta = [], []
    for qb in range(2):
        r = 1.0 / (row_pair(sums_a, h, 2 * qb) + row_pair(sums_b, h, 2 * qb))
        delta.append((row_pair(sums_a, h, 4 + 2 * qb) + row_pair(sums_b, h, 4 + 2 * qb)) * r)
        recip.append(r if keep is None else r * keep)
    for kb, qb, _ in blocks:
        p = e[eh, half(kb), half(qb)] * recip[qb]
        p_low[half(kb), half(qb)] = p.astype(jnp.bfloat16)
        ds_low[half(kb), half(qb)] = (p * (gp[eh, half(kb), half(qb)] - delta[qb])).astype(jnp.bfloat16)


def kernel(
    n_dp, n_ctx,
    q_hbm, k_hbm, v_hbm, g_hbm, gains,
    dq_hbm, dk_hbm, dv_hbm, gain_out,
    q, k, v, g, rq, rg, qn, kn, kt, rqn,
    e_own, gp_own, e_ahead, gp_ahead, p_low, ds_low,
    dk_acc, dv_acc, dq_own, dq_give, dq_take, dq_o, dk_o, dv_o,
    own_sums, right_sums, ahead_sums, left_sums,
    gain_part, gain_terms,
    load_sem, fwd_send, fwd_recv, own_send, own_recv, ahead_send, ahead_recv,
    dq_send, dq_recv, out_sem, gain_send, gain_recv,
):
    me_d, me_c = lax.axis_index("dp"), lax.axis_index("ctx")
    left, right = lax.rem(me_c + n_ctx - 1, n_ctx), lax.rem(me_c + 1, n_ctx)
    width = HEADS * HD // n_dp
    has_ahead = jnp.where(me_c < n_ctx - 1, 1.0, 0.0).astype(jnp.float32)
    has_behind = jnp.where(me_c > 0, 1.0, 0.0).astype(jnp.float32)

    loads = ((q_hbm, q), (g_hbm, g), (k_hbm, k), (v_hbm, v))

    def load(a, h):
        src, dst = loads[a]
        return pltpu.make_async_copy(src.at[0, :, pl.ds(h * HD, HD)], dst.at[h], load_sem.at[a, h])

    for h in range(HEADS):
        for a in range(4):
            load(a, h).start()

    barrier = pltpu.get_barrier_semaphore()

    n_in, n_y, n_z = n_dp // Z_HI, n_ctx // Z_LO, Z_HI * Z_LO
    me_in, me_y = lax.rem(me_d, n_in), lax.div(me_c, Z_LO)
    me_z = lax.div(me_d, n_in) * Z_LO + lax.rem(me_c, Z_LO)

    def device(axis, at):
        if axis == 0:
            return {"dp": me_d - me_in + at}
        if axis == 1:
            return {"ctx": lax.rem(me_c, Z_LO) + at * Z_LO}
        return {"dp": lax.div(at, Z_LO) * n_in + me_in, "ctx": me_y * Z_LO + lax.rem(at, Z_LO)}

    axes = ((n_in, me_in), (n_y, me_y), (n_z, me_z))

    for axis, (count, me) in enumerate(axes):

        @pl.loop(1, count)
        def _(i, axis=axis, count=count, me=me):
            pl.semaphore_signal(
                barrier, inc=1, device_id=device(axis, lax.rem(me + i, count)), device_id_type=MESH
            )

    for neighbour in (left, right):
        pl.semaphore_signal(barrier, inc=1, device_id={"ctx": neighbour}, device_id_type=MESH)
    pl.semaphore_wait(barrier, n_in + n_y + n_z - 1)

    def to_left(src, dst, send, recv):
        return pltpu.make_async_remote_copy(src, dst, send, recv, device_id={"ctx": left}, device_id_type=MESH)

    def to_right(src, dst, send, recv):
        return pltpu.make_async_remote_copy(src, dst, send, recv, device_id={"ctx": right}, device_id_type=MESH)

    def send_q(h):
        return to_left(q.at[h], rq.at[h], fwd_send.at[0, h], fwd_recv.at[0, h])

    def send_g(h):
        return to_left(g.at[h], rg.at[h], fwd_send.at[1, h], fwd_recv.at[1, h])

    def send_own_sums(h):
        return to_left(own_sums.at[h], right_sums.at[h], own_send.at[h], own_recv.at[h])

    def send_ahead_sums(h):
        return to_right(ahead_sums.at[h], left_sums.at[h], ahead_send.at[h], ahead_recv.at[h])

    def send_dq(h):
        return to_right(dq_give.at[h], dq_take.at[h], dq_send.at[h], dq_recv.at[h])

    def send_k():
        return to_right(k.at[LAST], rq.at[LAST], fwd_send.at[0, LAST], fwd_recv.at[0, LAST])

    def send_v():
        return to_right(v.at[LAST], rg.at[LAST], fwd_send.at[1, LAST], fwd_recv.at[1, LAST])

    def send_back(j):
        at = LAST + j
        return to_left(dq_give.at[at], dq_take.at[at], dq_send.at[at], dq_recv.at[at])

    def store(a, h):
        src, dst = ((dq_o, dq_hbm), (dk_o, dk_hbm), (dv_o, dv_hbm))[a]
        cols = pl.ds(pl.multiple_of(h * HD, HD), HD)
        return pltpu.make_async_copy(src.at[h], dst.at[0, :, cols], out_sem.at[a, h])

    def send_ahead(h):
        send_q(h).start()
        send_g(h).start()

    for h in range(HEADS):
        load(0, h).wait()
        load(1, h).wait()
        if h == 0:
            send_ahead(0)
    for h in range(HEADS):
        load(2, h).wait()
        load(3, h).wait()

    def gain_row(row, h):
        return gains[pl.ds(row, 1), pl.ds(pl.multiple_of(h * HD, HD), HD)]

    @pl.loop(0, HEADS)
    def _(h):
        for i in range(2):
            unit_q, _ = unit_rows(q[h, half(i), :])
            qn[h, half(i), :] = (unit_q * gain_row(0, h)).astype(jnp.bfloat16)
            unit_k, _ = unit_rows(k[h, half(i), :])
            normed = unit_k * gain_row(1, h)
            kn[h, half(i), :] = normed.astype(jnp.bfloat16)
            kt[h, :, half(i)] = normed.T.astype(jnp.bfloat16)
        exps_and_sums(h, OWN_BLOCKS, True, kn, h, v, qn, h, g, e_own, gp_own, h, own_sums)

        @pl.when(h < LAST)
        def _():
            send_own_sums(h).start()

        @pl.when(h == 1)
        def _():
            send_ahead(1)

    send_ahead(2)

    def finish_dq(h):
        send_dq(h).wait_recv()
        for i in range(2):
            grad = dq_own[h, half(i), :] + dq_take[h, half(i), :].astype(jnp.float32)
            unit_q, inv_q = unit_rows(q[h, half(i), :])
            dq_o[h, half(i), :] = norm_back(grad, unit_q, inv_q, gain_row(0, h))
        store(0, h).start()

    @pl.loop(0, LAST)
    def _(h):
        send_q(h).wait_recv()
        for i in range(2):
            unit_q, _ = unit_rows(rq[h, half(i), :])
            rqn[0, half(i), :] = (unit_q * gain_row(0, h)).astype(jnp.bfloat16)

        @pl.when(h == LAST - 1)
        def _():
            send_k().start()
            send_v().start()

        send_g(h).wait_recv()

        exps_and_sums(h, AHEAD_BLOCKS, False, kn, h, v, rqn, 0, rg, e_ahead, gp_ahead, 0, ahead_sums)
        ahead_sums[h] = ahead_sums[h] * has_ahead
        send_ahead_sums(h).start()

        send_own_sums(h).wait_recv()
        probs_and_grads(h, AHEAD_BLOCKS, e_ahead, gp_ahead, 0, right_sums, ahead_sums, has_ahead, p_low, ds_low)
        gain_q = jnp.zeros((1, HD), jnp.float32)
        for i in range(2):
            if i == 0:
                dqt = dot(kt[h], ds_low[:, half(0)])
            else:
                dqt = dot(kt[h, :, half(1)], ds_low[half(1), half(1)])
            grad = dqt.T * SCALE
            dq_give[h, half(i), :] = grad.astype(jnp.bfloat16)
            unit_q, _ = unit_rows(rq[h, half(i), :])
            gain_q += jnp.sum(grad * unit_q, axis=0, keepdims=True)
        gain_part[0, h, pl.ds(0, 1), :] = gain_q
        dk_acc[h, half(0), :] = dot(ds_low[half(0), half(0)], rqn[0, half(0), :])
        dk_acc[h, half(1), :] = dot(ds_low[half(1), :], rqn[0])
        dv_acc[h, half(0), :] = dot(p_low[half(0), half(0)], rg[h, half(0), :])
        dv_acc[h, half(1), :] = dot(p_low[half(1), :], rg[h])

    def own_part(h):
        send_ahead_sums(h).wait_recv()
        probs_and_grads(h, OWN_BLOCKS, e_own, gp_own, h, own_sums, left_sums, None, p_low, ds_low)
        gain_q = gain_part[0, h, pl.ds(0, 1), :]
        gain_k = jnp.zeros((1, HD), jnp.float32)
        for i in range(2):
            if i == 0:
                dk = dot(ds_low[half(0), :], qn[h])
                dv = dot(p_low[half(0), :], g[h])
                dqt = dot(kt[h, :, half(0)], ds_low[half(0), half(0)])
            else:
                dk = dot(ds_low[half(1), half(1)], qn[h, half(1), :])
                dv = dot(p_low[half(1), half(1)], g[h, half(1), :])
                dqt = dot(kt[h], ds_low[:, half(1)])
            dv_o[h, half(i), :] = (dv + dv_acc[h, half(i), :]).astype(jnp.bfloat16)
            grad_k = (dk + dk_acc[h, half(i), :]) * SCALE
            unit_k, inv_k = unit_rows(k[h, half(i), :])
            gain_k += jnp.sum(grad_k * unit_k, axis=0, keepdims=True)
            dk_o[h, half(i), :] = norm_back(grad_k, unit_k, inv_k, gain_row(1, h))
            grad_q = dqt.T * SCALE
            unit_q, _ = unit_rows(q[h, half(i), :])
            gain_q += jnp.sum(grad_q * unit_q, axis=0, keepdims=True)
            dq_own[h, half(i), :] = grad_q
        gain_part[0, h, pl.ds(0, 1), :] = gain_q
        gain_part[0, h, pl.ds(1, 1), :] = gain_k
        store(1, h).start()
        store(2, h).start()

    def last_part():
        h = LAST
        send_k().wait_recv()
        for i in range(2):
            unit_k, _ = unit_rows(rq[h, half(i), :])
            normed = unit_k * gain_row(1, h)
            rqn[0, half(i), :] = normed.astype(jnp.bfloat16)
            kt[HEADS, :, half(i)] = normed.T.astype(jnp.bfloat16)
        send_v().wait_recv()
        for earlier in range(LAST):
            send_dq(earlier).start()
        exps_and_sums(h, AHEAD_BLOCKS, False, rqn, 0, rg, qn, h, g, e_ahead, gp_ahead, 0, ahead_sums)
        ahead_sums[h] = ahead_sums[h] * has_behind
        probs_and_grads(h, AHEAD_BLOCKS, e_ahead, gp_ahead, 0, own_sums, ahead_sums, has_behind, p_low, ds_low)
        gain_q = jnp.zeros((1, HD), jnp.float32)
        gain_k = jnp.zeros((1, HD), jnp.float32)
        for i in range(2):
            if i == 0:
                dk = dot(ds_low[half(0), half(0)], qn[h, half(0), :])
                dv = dot(p_low[half(0), half(0)], g[h, half(0), :])
                dqt = dot(kt[HEADS], ds_low[:, half(0)])
            else:
                dk = dot(ds_low[half(1), :], qn[h])
                dv = dot(p_low[half(1), :], g[h])
                dqt = dot(kt[HEADS, :, half(1)], ds_low[half(1), half(1)])
            grad_k = dk * SCALE
            unit_k, _ = unit_rows(rq[h, half(i), :])
            gain_k += jnp.sum(grad_k * unit_k, axis=0, keepdims=True)
            dq_give[h, half(i), :] = grad_k.astype(jnp.bfloat16)
            dq_give[h + 1, half(i), :] = dv.astype(jnp.bfloat16)
            dq_own[h, half(i), :] = dqt.T * SCALE
        send_back(0).start()
        send_back(1).start()
        probs_and_grads(h, OWN_BLOCKS, e_own, gp_own, h, own_sums, ahead_sums, None, p_low, ds_low)
        for i in range(2):
            if i == 0:
                dk = dot(ds_low[half(0), :], qn[h])
                dv = dot(p_low[half(0), :], g[h])
                dqt = dot(kt[h, :, half(0)], ds_low[half(0), half(0)])
            else:
                dk = dot(ds_low[half(1), half(1)], qn[h, half(1), :])
                dv = dot(p_low[half(1), half(1)], g[h, half(1), :])
                dqt = dot(kt[h], ds_low[:, half(1)])
            dv_acc[h, half(i), :] = dv
            grad_k = dk * SCALE
            dk_acc[h, half(i), :] = grad_k
            unit_k, _ = unit_rows(k[h, half(i), :])
            gain_k += jnp.sum(grad_k * unit_k, axis=0, keepdims=True)
            grad_q = dq_own[h, half(i), :] + dqt.T * SCALE
            unit_q, inv_q = unit_rows(q[h, half(i), :])
            gain_q += jnp.sum(grad_q * unit_q, axis=0, keepdims=True)
            dq_o[h, half(i), :] = norm_back(grad_q, unit_q, inv_q, gain_row(0, h))
        gain_part[0, h, pl.ds(0, 1), :] = gain_q
        gain_part[0, h, pl.ds(1, 1), :] = gain_k
        store(0, h).start()

    def finish_last():
        h = LAST
        send_back(0).wait_recv()
        send_back(1).wait_recv()
        for i in range(2):
            grad_k = dk_acc[h, half(i), :] + dq_take[h, half(i), :].astype(jnp.float32)
            unit_k, inv_k = unit_rows(k[h, half(i), :])
            dk_o[h, half(i), :] = norm_back(grad_k, unit_k, inv_k, gain_row(1, h))
            dv = dv_acc[h, half(i), :] + dq_take[h + 1, half(i), :].astype(jnp.float32)
            dv_o[h, half(i), :] = dv.astype(jnp.bfloat16)
        store(1, h).start()
        store(2, h).start()

    @pl.loop(0, LAST)
    def _(h):
        @pl.when(h == LAST - 1)
        def _():
            last_part()

        own_part(h)

    def send_gain(axis, i):
        count, me = axes[axis]
        return pltpu.make_async_remote_copy(
            gain_part.at[axis], gain_terms.at[axis, me], gain_send.at[axis, i], gain_recv.at[axis, i],
            device_id=device(axis, lax.rem(me + i, count)), device_id_type=MESH,
        )

    def start_gains(axis):
        @pl.loop(1, axes[axis][0])
        def _(i):
            send_gain(axis, i).start()

    def sum_gains(axis):
        count, me = axes[axis]
        gain_terms[axis, me] = gain_part[axis]

        @pl.loop(1, count)
        def _(i):
            at = gain_terms.at[axis, lax.rem(me + count - i, count)]
            pltpu.make_async_remote_copy(
                at, at, gain_send.at[axis, i], gain_recv.at[axis, i],
                device_id=device(axis, lax.rem(me + i, count)), device_id_type=MESH,
            ).wait_recv()

        total = gain_terms[axis, 0]
        for i in range(1, count):
            total = total + gain_terms[axis, i]
        gain_part[axis + 1] = total

    start_gains(0)
    sum_gains(0)
    start_gains(1)
    sum_gains(1)
    start_gains(2)

    @pl.loop(0, LAST)
    def _(h):
        finish_dq(h)

    finish_last()

    sum_gains(2)
    per_head = HD // width
    mine = gain_part[3, lax.div(me_d, per_head)]
    for j in range(per_head):

        @pl.when(lax.rem(me_d, per_head) == j)
        def _(j=j):
            gain_out[...] = mine[:, j * width : (j + 1) * width]

    @pl.loop(0, LAST)
    def _(h):
        send_q(h).wait_send()
        send_g(h).wait_send()
        send_own_sums(h).wait_send()
        send_ahead_sums(h).wait_send()
        send_dq(h).wait_send()

    send_k().wait_send()
    send_v().wait_send()
    send_back(0).wait_send()
    send_back(1).wait_send()

    @pl.loop(0, HEADS)
    def _(h):
        for a in range(3):
            store(a, h).wait()

    for axis in range(3):

        @pl.loop(1, axes[axis][0])
        def _(i, axis=axis):
            send_gain(axis, i).wait_send()


def hand_out(*refs):
    sem = refs[8]
    copies = [pltpu.make_async_copy(refs[i], refs[4 + i], sem.at[i]) for i in range(4)]
    for copy in copies:
        copy.start()
    for copy in copies:
        copy.wait()


def per_device(n_dp, n_ctx, queries, keys, values, grad_out, gains):
    rows = queries.shape[1]
    most = max(n_dp // Z_HI, n_ctx // Z_LO, Z_HI * Z_LO)
    low, wide = jnp.bfloat16, jnp.float32
    heads_low = pltpu.VMEM((HEADS, rows, HD), low)
    sums = pltpu.VMEM((HEADS, 8, HD), wide)
    dma = pltpu.SemaphoreType.DMA
    any_space = pl.BlockSpec(memory_space=pl.ANY)
    vmem = pl.BlockSpec(memory_space=pltpu.VMEM)
    big = pltpu.VMEM(queries.shape, low)
    hbm = pl.BlockSpec(memory_space=pltpu.HBM)
    results = pl.pallas_call(
        functools.partial(kernel, n_dp, n_ctx),
        out_shape=(big, big, big, pltpu.VMEM((2, HEADS * HD // n_dp), wide)),
        in_specs=[any_space] * 4 + [vmem],
        out_specs=(vmem,) * 4,
        scratch_shapes=[heads_low] * 8
        + [
            pltpu.VMEM((HEADS + 1, HD, rows), low),
            pltpu.VMEM((1, rows, HD), low),
            pltpu.VMEM((HEADS, rows, rows), wide),
            pltpu.VMEM((HEADS, rows, rows), wide),
            pltpu.VMEM((1, rows, rows), wide),
            pltpu.VMEM((1, rows, rows), wide),
            pltpu.VMEM((rows, rows), low),
            pltpu.VMEM((rows, rows), low),
            pltpu.VMEM((HEADS, rows, HD), wide),
            pltpu.VMEM((HEADS, rows, HD), wide),
            pltpu.VMEM((HEADS, rows, HD), wide),
        ]
        + [pltpu.VMEM((HEADS + 1, rows, HD), low)] * 2
        + [heads_low] * 3
        + [sums] * 4
        + [
            pltpu.VMEM((4, HEADS, 2, HD), wide),
            pltpu.VMEM((3, most, HEADS, 2, HD), wide),
            dma((4, HEADS)),
            dma((2, HEADS)),
            dma((2, HEADS)),
            dma((HEADS,)),
            dma((HEADS,)),
            dma((HEADS,)),
            dma((HEADS,)),
            dma((HEADS + 1,)),
            dma((HEADS + 1,)),
            dma((3, HEADS)),
            dma((3, most)),
            dma((3, most)),
        ],
        compiler_params=pltpu.CompilerParams(
            collective_id=0, has_side_effects=True, vmem_limit_bytes=60 * 1024 * 1024
        ),
    )(queries, keys, values, grad_out, gains)
    return pl.pallas_call(
        hand_out,
        out_shape=tuple(jax.ShapeDtypeStruct(r.shape, r.dtype) for r in results),
        in_specs=[any_space] * 4,
        out_specs=(hbm,) * 4,
        scratch_shapes=[dma((4,))],
        compiler_params=pltpu.CompilerParams(vmem_limit_bytes=2 * 1024 * 1024),
    )(*results)


def solution(mesh):
    placed = (
        P("dp", "ctx", None),
        P("dp", "ctx", None),
        P("dp", "ctx", None),
        P("dp", "ctx", None),
        P(),
    )
    return jax.shard_map(
        functools.partial(per_device, mesh.shape["dp"], mesh.shape["ctx"]),
        mesh=mesh,
        in_specs=placed,
        out_specs=(P("dp", "ctx", None), P("dp", "ctx", None), P("dp", "ctx", None), P(None, "dp")),
        check_vma=False,
    )
```

```python
import functools
import math

import jax
import jax.numpy as jnp
from jax import lax
from jax.experimental import pallas as pl
from jax.experimental.pallas import tpu as pltpu
from jax.sharding import PartitionSpec as P

HEADS = 4
HD = 128
EPS = 1e-06
HALF = 256
LAST = HEADS - 1
Z_HI, Z_LO = 2, 4
SCALE = 1.0 / math.sqrt(HD)
EXP2_SCALE = SCALE * math.log2(math.e)
MESH = pl.DeviceIdType.MESH

OWN_BLOCKS = ((0, 0, True), (0, 1, False), (1, 1, True))
AHEAD_BLOCKS = ((0, 0, True), (1, 0, False), (1, 1, True))


def half(i):
    return pl.ds(i * HALF, HALF)


def dot_nt(a, b):
    return lax.dot_general(a, b, (((1,), (1,)), ((), ())), preferred_element_type=jnp.float32)


def dot(a, b):
    return jnp.dot(a, b, preferred_element_type=jnp.float32)


def unit_rows(x):
    wide = x.astype(jnp.float32)
    inverse = lax.rsqrt(jnp.mean(wide * wide, axis=1, keepdims=True) + EPS)
    return wide * inverse, inverse


def norm_back(grad, unit, inverse, gain):
    scaled = grad * gain
    mean_term = jnp.mean(scaled * unit, axis=1, keepdims=True)
    return (inverse * (scaled - unit * mean_term)).astype(jnp.bfloat16)


def exps_and_sums(h, blocks, own, kn, kh, v, qn, qh, g, e, gp, eh, sums):
    total = [None, None]
    weighted = [None, None]
    for kb, qb, edge in blocks:
        s = dot_nt(kn[kh, half(kb), :], qn[qh, half(qb), :])
        ex = jnp.exp2(s * EXP2_SCALE)
        if edge:
            key = lax.broadcasted_iota(jnp.int32, (HALF, HALF), 0)
            query = lax.broadcasted_iota(jnp.int32, (HALF, HALF), 1)
            ex = jnp.where(key <= query if own else key > query, ex, 0.0)
        gr = dot_nt(v[h, half(kb), :], g[h, half(qb), :])
        e[eh, half(kb), half(qb)] = ex
        gp[eh, half(kb), half(qb)] = gr
        t = jnp.sum(ex, axis=0, keepdims=True)
        w = jnp.sum(ex * gr, axis=0, keepdims=True)
        total[qb] = t if total[qb] is None else total[qb] + t
        weighted[qb] = w if weighted[qb] is None else weighted[qb] + w
    for qb in range(2):
        for i in range(2):
            sums[h, pl.ds(2 * qb + i, 1), :] = total[qb][:, i * HD : (i + 1) * HD]
            sums[h, pl.ds(4 + 2 * qb + i, 1), :] = weighted[qb][:, i * HD : (i + 1) * HD]


def row_pair(ref, h, first):
    return jnp.concatenate([ref[h, pl.ds(first, 1), :], ref[h, pl.ds(first + 1, 1), :]], axis=1)


def probs_and_grads(h, blocks, e, gp, eh, sums_a, sums_b, keep, p_low, ds_low):
    recip, delta = [], []
    for qb in range(2):
        r = 1.0 / (row_pair(sums_a, h, 2 * qb) + row_pair(sums_b, h, 2 * qb))
        delta.append((row_pair(sums_a, h, 4 + 2 * qb) + row_pair(sums_b, h, 4 + 2 * qb)) * r)
        recip.append(r if keep is None else r * keep)
    for kb, qb, _ in blocks:
        p = e[eh, half(kb), half(qb)] * recip[qb]
        p_low[half(kb), half(qb)] = p.astype(jnp.bfloat16)
        ds_low[half(kb), half(qb)] = (p * (gp[eh, half(kb), half(qb)] - delta[qb])).astype(jnp.bfloat16)


def kernel(
    n_dp, n_ctx,
    q_hbm, k_hbm, v_hbm, g_hbm, gains,
    dq_hbm, dk_hbm, dv_hbm, gain_out,
    q, k, v, g, rq, rg, qn, kn, kt, rqn,
    e_own, gp_own, e_ahead, gp_ahead, p_low, ds_low,
    dk_acc, dv_acc, dq_own, dq_give, dq_take, dq_o, dk_o, dv_o,
    own_sums, right_sums, ahead_sums, left_sums,
    gain_part, gain_terms,
    load_sem, fwd_send, fwd_recv, own_send, own_recv, ahead_send, ahead_recv,
    dq_send, dq_recv, out_sem, gain_send, gain_recv,
):
    me_d, me_c = lax.axis_index("dp"), lax.axis_index("ctx")
    left, right = lax.rem(me_c + n_ctx - 1, n_ctx), lax.rem(me_c + 1, n_ctx)
    width = HEADS * HD // n_dp
    has_ahead = jnp.where(me_c < n_ctx - 1, 1.0, 0.0).astype(jnp.float32)
    has_behind = jnp.where(me_c > 0, 1.0, 0.0).astype(jnp.float32)

    loads = ((q_hbm, q), (g_hbm, g), (k_hbm, k), (v_hbm, v))

    def load(a, h):
        src, dst = loads[a]
        return pltpu.make_async_copy(src.at[0, :, pl.ds(h * HD, HD)], dst.at[h], load_sem.at[a, h])

    for h in range(HEADS):
        for a in range(4):
            load(a, h).start()

    barrier = pltpu.get_barrier_semaphore()

    n_in, n_y, n_z = n_dp // Z_HI, n_ctx // Z_LO, Z_HI * Z_LO
    me_in, me_y = lax.rem(me_d, n_in), lax.div(me_c, Z_LO)
    me_z = lax.div(me_d, n_in) * Z_LO + lax.rem(me_c, Z_LO)

    def device(axis, at):
        if axis == 0:
            return {"dp": me_d - me_in + at}
        if axis == 1:
            return {"ctx": lax.rem(me_c, Z_LO) + at * Z_LO}
        return {"dp": lax.div(at, Z_LO) * n_in + me_in, "ctx": me_y * Z_LO + lax.rem(at, Z_LO)}

    axes = ((n_in, me_in), (n_y, me_y), (n_z, me_z))

    for axis, (count, me) in enumerate(axes):

        @pl.loop(1, count)
        def _(i, axis=axis, count=count, me=me):
            pl.semaphore_signal(
                barrier, inc=1, device_id=device(axis, lax.rem(me + i, count)), device_id_type=MESH
            )

    for neighbour in (left, right):
        pl.semaphore_signal(barrier, inc=1, device_id={"ctx": neighbour}, device_id_type=MESH)
    pl.semaphore_wait(barrier, n_in + n_y + n_z - 1)

    def to_left(src, dst, send, recv):
        return pltpu.make_async_remote_copy(src, dst, send, recv, device_id={"ctx": left}, device_id_type=MESH)

    def to_right(src, dst, send, recv):
        return pltpu.make_async_remote_copy(src, dst, send, recv, device_id={"ctx": right}, device_id_type=MESH)

    def send_q(h):
        return to_left(q.at[h], rq.at[h], fwd_send.at[0, h], fwd_recv.at[0, h])

    def send_g(h):
        return to_left(g.at[h], rg.at[h], fwd_send.at[1, h], fwd_recv.at[1, h])

    def send_own_sums(h):
        return to_left(own_sums.at[h], right_sums.at[h], own_send.at[h], own_recv.at[h])

    def send_ahead_sums(h):
        return to_right(ahead_sums.at[h], left_sums.at[h], ahead_send.at[h], ahead_recv.at[h])

    def send_dq(h):
        return to_right(dq_give.at[h], dq_take.at[h], dq_send.at[h], dq_recv.at[h])

    def send_k():
        return to_right(k.at[LAST], rq.at[LAST], fwd_send.at[0, LAST], fwd_recv.at[0, LAST])

    def send_v():
        return to_right(v.at[LAST], rg.at[LAST], fwd_send.at[1, LAST], fwd_recv.at[1, LAST])

    def send_back(j):
        at = LAST + j
        return to_left(dq_give.at[at], dq_take.at[at], dq_send.at[at], dq_recv.at[at])

    def store(a, h):
        src, dst = ((dq_o, dq_hbm), (dk_o, dk_hbm), (dv_o, dv_hbm))[a]
        cols = pl.ds(pl.multiple_of(h * HD, HD), HD)
        return pltpu.make_async_copy(src.at[h], dst.at[0, :, cols], out_sem.at[a, h])

    def send_ahead(h):
        send_q(h).start()
        send_g(h).start()

    for h in range(HEADS):
        load(0, h).wait()
        load(1, h).wait()
        if h == 0:
            send_ahead(0)
    for h in range(HEADS):
        load(2, h).wait()
        load(3, h).wait()

    def gain_row(row, h):
        return gains[pl.ds(row, 1), pl.ds(pl.multiple_of(h * HD, HD), HD)]

    @pl.loop(0, HEADS)
    def _(h):
        for i in range(2):
            unit_q, _ = unit_rows(q[h, half(i), :])
            qn[h, half(i), :] = (unit_q * gain_row(0, h)).astype(jnp.bfloat16)
            unit_k, _ = unit_rows(k[h, half(i), :])
            normed = unit_k * gain_row(1, h)
            kn[h, half(i), :] = normed.astype(jnp.bfloat16)
            kt[h, :, half(i)] = normed.T.astype(jnp.bfloat16)
        exps_and_sums(h, OWN_BLOCKS, True, kn, h, v, qn, h, g, e_own, gp_own, h, own_sums)

        @pl.when(h < LAST)
        def _():
            send_own_sums(h).start()

        @pl.when(h == 1)
        def _():
            send_ahead(1)

    send_ahead(2)

    def finish_dq(h):
        send_dq(h).wait_recv()
        for i in range(2):
            grad = dq_own[h, half(i), :] + dq_take[h, half(i), :].astype(jnp.float32)
            unit_q, inv_q = unit_rows(q[h, half(i), :])
            dq_o[h, half(i), :] = norm_back(grad, unit_q, inv_q, gain_row(0, h))
        store(0, h).start()

    @pl.loop(0, LAST)
    def _(h):
        send_q(h).wait_recv()
        for i in range(2):
            unit_q, _ = unit_rows(rq[h, half(i), :])
            rqn[0, half(i), :] = (unit_q * gain_row(0, h)).astype(jnp.bfloat16)

        @pl.when(h == LAST - 1)
        def _():
            send_k().start()
            send_v().start()

        send_g(h).wait_recv()

        exps_and_sums(h, AHEAD_BLOCKS, False, kn, h, v, rqn, 0, rg, e_ahead, gp_ahead, 0, ahead_sums)
        ahead_sums[h] = ahead_sums[h] * has_ahead
        send_ahead_sums(h).start()

        send_own_sums(h).wait_recv()
        probs_and_grads(h, AHEAD_BLOCKS, e_ahead, gp_ahead, 0, right_sums, ahead_sums, has_ahead, p_low, ds_low)
        gain_q = jnp.zeros((1, HD), jnp.float32)
        for i in range(2):
            if i == 0:
                dqt = dot(kt[h], ds_low[:, half(0)])
            else:
                dqt = dot(kt[h, :, half(1)], ds_low[half(1), half(1)])
            grad = dqt.T * SCALE
            dq_give[h, half(i), :] = grad.astype(jnp.bfloat16)
            unit_q, _ = unit_rows(rq[h, half(i), :])
            gain_q += jnp.sum(grad * unit_q, axis=0, keepdims=True)
        gain_part[0, h, pl.ds(0, 1), :] = gain_q
        dk_acc[h, half(0), :] = dot(ds_low[half(0), half(0)], rqn[0, half(0), :])
        dk_acc[h, half(1), :] = dot(ds_low[half(1), :], rqn[0])
        dv_acc[h, half(0), :] = dot(p_low[half(0), half(0)], rg[h, half(0), :])
        dv_acc[h, half(1), :] = dot(p_low[half(1), :], rg[h])

    def own_part(h):
        send_ahead_sums(h).wait_recv()
        probs_and_grads(h, OWN_BLOCKS, e_own, gp_own, h, own_sums, left_sums, None, p_low, ds_low)
        gain_q = gain_part[0, h, pl.ds(0, 1), :]
        gain_k = jnp.zeros((1, HD), jnp.float32)
        for i in range(2):
            if i == 0:
                dk = dot(ds_low[half(0), :], qn[h])
                dv = dot(p_low[half(0), :], g[h])
                dqt = dot(kt[h, :, half(0)], ds_low[half(0), half(0)])
            else:
                dk = dot(ds_low[half(1), half(1)], qn[h, half(1), :])
                dv = dot(p_low[half(1), half(1)], g[h, half(1), :])
                dqt = dot(kt[h], ds_low[:, half(1)])
            dv_o[h, half(i), :] = (dv + dv_acc[h, half(i), :]).astype(jnp.bfloat16)
            grad_k = (dk + dk_acc[h, half(i), :]) * SCALE
            unit_k, inv_k = unit_rows(k[h, half(i), :])
            gain_k += jnp.sum(grad_k * unit_k, axis=0, keepdims=True)
            dk_o[h, half(i), :] = norm_back(grad_k, unit_k, inv_k, gain_row(1, h))
            grad_q = dqt.T * SCALE
            unit_q, _ = unit_rows(q[h, half(i), :])
            gain_q += jnp.sum(grad_q * unit_q, axis=0, keepdims=True)
            dq_own[h, half(i), :] = grad_q
        gain_part[0, h, pl.ds(0, 1), :] = gain_q
        gain_part[0, h, pl.ds(1, 1), :] = gain_k
        store(1, h).start()
        store(2, h).start()

    def last_part():
        h = LAST
        send_k().wait_recv()
        for i in range(2):
            unit_k, _ = unit_rows(rq[h, half(i), :])
            normed = unit_k * gain_row(1, h)
            rqn[0, half(i), :] = normed.astype(jnp.bfloat16)
            kt[HEADS, :, half(i)] = normed.T.astype(jnp.bfloat16)
        send_v().wait_recv()
        for earlier in range(LAST):
            send_dq(earlier).start()
        exps_and_sums(h, AHEAD_BLOCKS, False, rqn, 0, rg, qn, h, g, e_ahead, gp_ahead, 0, ahead_sums)
        ahead_sums[h] = ahead_sums[h] * has_behind
        probs_and_grads(h, AHEAD_BLOCKS, e_ahead, gp_ahead, 0, own_sums, ahead_sums, has_behind, p_low, ds_low)
        gain_q = jnp.zeros((1, HD), jnp.float32)
        gain_k = jnp.zeros((1, HD), jnp.float32)
        for i in range(2):
            if i == 0:
                dk = dot(ds_low[half(0), half(0)], qn[h, half(0), :])
                dv = dot(p_low[half(0), half(0)], g[h, half(0), :])
                dqt = dot(kt[HEADS], ds_low[:, half(0)])
            else:
                dk = dot(ds_low[half(1), :], qn[h])
                dv = dot(p_low[half(1), :], g[h])
                dqt = dot(kt[HEADS, :, half(1)], ds_low[half(1), half(1)])
            grad_k = dk * SCALE
            unit_k, _ = unit_rows(rq[h, half(i), :])
            gain_k += jnp.sum(grad_k * unit_k, axis=0, keepdims=True)
            dq_give[h, half(i), :] = grad_k.astype(jnp.bfloat16)
            dq_give[h + 1, half(i), :] = dv.astype(jnp.bfloat16)
            dq_own[h, half(i), :] = dqt.T * SCALE
        send_back(0).start()
        send_back(1).start()
        probs_and_grads(h, OWN_BLOCKS, e_own, gp_own, h, own_sums, ahead_sums, None, p_low, ds_low)
        for i in range(2):
            if i == 0:
                dk = dot(ds_low[half(0), :], qn[h])
                dv = dot(p_low[half(0), :], g[h])
                dqt = dot(kt[h, :, half(0)], ds_low[half(0), half(0)])
            else:
                dk = dot(ds_low[half(1), half(1)], qn[h, half(1), :])
                dv = dot(p_low[half(1), half(1)], g[h, half(1), :])
                dqt = dot(kt[h], ds_low[:, half(1)])
            dv_acc[h, half(i), :] = dv
            grad_k = dk * SCALE
            dk_acc[h, half(i), :] = grad_k
            unit_k, _ = unit_rows(k[h, half(i), :])
            gain_k += jnp.sum(grad_k * unit_k, axis=0, keepdims=True)
            grad_q = dq_own[h, half(i), :] + dqt.T * SCALE
            unit_q, _ = unit_rows(q[h, half(i), :])
            gain_q += jnp.sum(grad_q * unit_q, axis=0, keepdims=True)
            dq_own[h, half(i), :] = grad_q
        gain_part[0, h, pl.ds(0, 1), :] = gain_q
        gain_part[0, h, pl.ds(1, 1), :] = gain_k

    def finish_last():
        h = LAST
        for i in range(2):
            unit_q, inv_q = unit_rows(q[h, half(i), :])
            dq_o[h, half(i), :] = norm_back(dq_own[h, half(i), :], unit_q, inv_q, gain_row(0, h))
        store(0, h).start()
        send_back(0).wait_recv()
        send_back(1).wait_recv()
        for i in range(2):
            grad_k = dk_acc[h, half(i), :] + dq_take[h, half(i), :].astype(jnp.float32)
            unit_k, inv_k = unit_rows(k[h, half(i), :])
            dk_o[h, half(i), :] = norm_back(grad_k, unit_k, inv_k, gain_row(1, h))
            dv = dv_acc[h, half(i), :] + dq_take[h + 1, half(i), :].astype(jnp.float32)
            dv_o[h, half(i), :] = dv.astype(jnp.bfloat16)
        store(1, h).start()
        store(2, h).start()

    @pl.loop(0, LAST)
    def _(h):
        @pl.when(h == LAST - 1)
        def _():
            last_part()

        own_part(h)

    def send_gain(axis, i):
        count, me = axes[axis]
        return pltpu.make_async_remote_copy(
            gain_part.at[axis], gain_terms.at[axis, me], gain_send.at[axis, i], gain_recv.at[axis, i],
            device_id=device(axis, lax.rem(me + i, count)), device_id_type=MESH,
        )

    def start_gains(axis):
        count = axes[axis][0]
        for i in sorted(range(1, count), key=lambda i: abs(i - count // 2)):
            send_gain(axis, i).start()

    def sum_gains(axis):
        count, me = axes[axis]
        gain_terms[axis, me] = gain_part[axis]

        @pl.loop(1, count)
        def _(i):
            at = gain_terms.at[axis, lax.rem(me + count - i, count)]
            pltpu.make_async_remote_copy(
                at, at, gain_send.at[axis, i], gain_recv.at[axis, i],
                device_id=device(axis, lax.rem(me + i, count)), device_id_type=MESH,
            ).wait_recv()

        total = gain_terms[axis, 0]
        for i in range(1, count):
            total = total + gain_terms[axis, i]
        gain_part[axis + 1] = total

    start_gains(0)
    sum_gains(0)
    start_gains(1)
    sum_gains(1)
    start_gains(2)

    @pl.loop(0, LAST)
    def _(h):
        finish_dq(h)

    finish_last()

    sum_gains(2)
    per_head = HD // width
    mine = gain_part[3, lax.div(me_d, per_head)]
    for j in range(per_head):

        @pl.when(lax.rem(me_d, per_head) == j)
        def _(j=j):
            gain_out[...] = mine[:, j * width : (j + 1) * width]

    @pl.loop(0, LAST)
    def _(h):
        send_q(h).wait_send()
        send_g(h).wait_send()
        send_own_sums(h).wait_send()
        send_ahead_sums(h).wait_send()
        send_dq(h).wait_send()

    send_k().wait_send()
    send_v().wait_send()
    send_back(0).wait_send()
    send_back(1).wait_send()

    @pl.loop(0, HEADS)
    def _(h):
        for a in range(3):
            store(a, h).wait()

    for axis in range(3):

        @pl.loop(1, axes[axis][0])
        def _(i, axis=axis):
            send_gain(axis, i).wait_send()


def hand_out(*refs):
    sem = refs[8]
    copies = [pltpu.make_async_copy(refs[i], refs[4 + i], sem.at[i]) for i in range(4)]
    for copy in copies:
        copy.start()
    for copy in copies:
        copy.wait()


def per_device(n_dp, n_ctx, queries, keys, values, grad_out, gains):
    rows = queries.shape[1]
    most = max(n_dp // Z_HI, n_ctx // Z_LO, Z_HI * Z_LO)
    low, wide = jnp.bfloat16, jnp.float32
    heads_low = pltpu.VMEM((HEADS, rows, HD), low)
    sums = pltpu.VMEM((HEADS, 8, HD), wide)
    dma = pltpu.SemaphoreType.DMA
    any_space = pl.BlockSpec(memory_space=pl.ANY)
    vmem = pl.BlockSpec(memory_space=pltpu.VMEM)
    big = pltpu.VMEM(queries.shape, low)
    hbm = pl.BlockSpec(memory_space=pltpu.HBM)
    results = pl.pallas_call(
        functools.partial(kernel, n_dp, n_ctx),
        out_shape=(big, big, big, pltpu.VMEM((2, HEADS * HD // n_dp), wide)),
        in_specs=[any_space] * 4 + [vmem],
        out_specs=(vmem,) * 4,
        scratch_shapes=[heads_low] * 8
        + [
            pltpu.VMEM((HEADS + 1, HD, rows), low),
            pltpu.VMEM((1, rows, HD), low),
            pltpu.VMEM((HEADS, rows, rows), wide),
            pltpu.VMEM((HEADS, rows, rows), wide),
            pltpu.VMEM((1, rows, rows), wide),
            pltpu.VMEM((1, rows, rows), wide),
            pltpu.VMEM((rows, rows), low),
            pltpu.VMEM((rows, rows), low),
            pltpu.VMEM((HEADS, rows, HD), wide),
            pltpu.VMEM((HEADS, rows, HD), wide),
            pltpu.VMEM((HEADS, rows, HD), wide),
        ]
        + [pltpu.VMEM((HEADS + 1, rows, HD), low)] * 2
        + [heads_low] * 3
        + [sums] * 4
        + [
            pltpu.VMEM((4, HEADS, 2, HD), wide),
            pltpu.VMEM((3, most, HEADS, 2, HD), wide),
            dma((4, HEADS)),
            dma((2, HEADS)),
            dma((2, HEADS)),
            dma((HEADS,)),
            dma((HEADS,)),
            dma((HEADS,)),
            dma((HEADS,)),
            dma((HEADS + 1,)),
            dma((HEADS + 1,)),
            dma((3, HEADS)),
            dma((3, most)),
            dma((3, most)),
        ],
        compiler_params=pltpu.CompilerParams(
            collective_id=0, has_side_effects=True, vmem_limit_bytes=60 * 1024 * 1024
        ),
    )(queries, keys, values, grad_out, gains)
    return pl.pallas_call(
        hand_out,
        out_shape=tuple(jax.ShapeDtypeStruct(r.shape, r.dtype) for r in results),
        in_specs=[any_space] * 4,
        out_specs=(hbm,) * 4,
        scratch_shapes=[dma((4,))],
        compiler_params=pltpu.CompilerParams(vmem_limit_bytes=2 * 1024 * 1024),
    )(*results)


def solution(mesh):
    placed = (
        P("dp", "ctx", None),
        P("dp", "ctx", None),
        P("dp", "ctx", None),
        P("dp", "ctx", None),
        P(),
    )
    return jax.shard_map(
        functools.partial(per_device, mesh.shape["dp"], mesh.shape["ctx"]),
        mesh=mesh,
        in_specs=placed,
        out_specs=(P("dp", "ctx", None), P("dp", "ctx", None), P("dp", "ctx", None), P(None, "dp")),
        check_vma=False,
    )
```
